256 devices in a mesh: rep: 16 (over y_hi, x, core), node: 8 (over z), tp: 2 (over y_lo).
Axes of the slice: x: 4, y: 4 (y_hi: 2, y_lo: 2; y = y_hi * 2 + y_lo), z: 8, core: 2. Of those that a mesh axis runs over, the one named last changes fastest.
Arguments:
- hidden_states: bfloat16 [32768, 8192], P(('rep', 'node'), 'tp'), may hold values from -134 to 134
- norm_gain: bfloat16 [8192], P('tp'), may hold values from 0.5 to 1.5
- value_weight: bfloat16 [8192, 512], P(('rep', 'node'), 'tp'), may hold values from -0.0625 to 0.0625
- queries: bfloat16 [32768, 4096], P(('rep', 'node'), 'tp'), may hold values from -88 to 88
- keys: bfloat16 [32768, 512], P(('rep', 'node'), 'tp'), may hold values from -4.4 to 4.4
- readout: float32 [4096], P('tp'), may hold values from -1.5 to 1.5
- targets: float32 [32768], P(('rep', 'node')), may hold values from -4 to 4
- scored: int32 [32768], P(('rep', 'node')), may hold values 0 or 1
Outputs:
- values: float32 [32768], P(('rep', 'node'))
- grad_input: bfloat16 [32768, 8192], P(('rep', 'node'), 'tp')
- grad_weight: float32 [8192, 512], P(('rep', 'node'), 'tp')
- grad_gain: float32 [8192], P('tp')
- grad_readout: float32 [4096], P('tp')
- grad_log_scale: float32 [32768], P(('rep', 'node'))
The draws below stay inside these ranges and needn't reach their ends.
All inputs are finite; a program needn't handle non-finite values. No bound on the sum of `scored` on one device may be relied on, other than what follows from the above.
Results may differ from the reference program's by a relative error of at most 0.015.
Values may be sent and summed in bfloat16 or wider, within the bound.
No kernel may reach another device: no remote copies, remote signals or barrier semaphores. Data moves between devices by JAX's collectives and lax.ppermute only.
A program may use at most 128 MiB of HBM per device.

```python
import math
import jax
import jax.numpy as jnp
from jax import lax

D = 8192
HD = 128
GROUP = 8
KVH = 4
TOK_DEV = 256
QH = 32
TOKENS = 32768


def shared_keys(key):
    return jax.random.truncated_normal(key, -4.0, 4.0, (TOKENS, KVH, HD), jnp.float32)


def draw_keys(key, part):
    base = shared_keys(key)
    return base.reshape(TOKENS, KVH * HD).astype(jnp.bfloat16)


def draw_queries(key, part):
    key = jax.random.fold_in(key, 5)
    fresh = jax.random.truncated_normal(key, -4.0, 4.0, (TOKENS, KVH, GROUP, HD), jnp.float32)
    return fresh.reshape(TOKENS, KVH * GROUP * HD).astype(jnp.bfloat16)


def draw_hidden_states(key, part):
    key = jax.random.fold_in(key, 11)
    values = jax.random.truncated_normal(key, -4.0, 4.0, (TOKENS, D), jnp.float32)
    return values.astype(jnp.bfloat16)


def touch_ends(array, own_key, least, high):
    longest = array.shape.index(max(array.shape))
    spots = []
    for shift in (0, 1):
        where = [jax.random.randint(jax.random.fold_in(own_key, axis), (), 0, length) for axis, length in enumerate(array.shape)]
        where[longest] = (where[longest] + shift) % array.shape[longest]
        spots.append(tuple(where))
    return array.at[spots[0]].set(least).at[spots[1]].set(high)


def steps_of(own_key, extent, cuts, low, top_value):
    level = 1.0
    for dim, parts in cuts:
        heights = jax.random.uniform(jax.random.fold_in(jax.random.fold_in(own_key, 6), dim), (parts,), jnp.float32, low / len(cuts), top_value / len(cuts))
        level = level * jnp.repeat(jnp.exp(heights), extent[dim] // parts).reshape((-1,) + (1,) * (len(extent) - 1 - dim))
    return level


def normal_values(stream_key, dims, scale, bound, split=(), dtype=jnp.bfloat16):
    result = scale * jax.random.normal(stream_key, dims, jnp.float32)
    if split:
        result = result * steps_of(stream_key, dims, split, -0.22, 0.18)
    return jnp.clip(result, -bound, bound).astype(dtype)


def setup_inputs(seed: int = 0) -> dict:
    key_of = jax.random.split(jax.random.key(seed), 9)
    hidden_states = draw_hidden_states(jax.random.fold_in(key_of[8], 71), 0)
    norm_gain = jnp.clip(1.0 + 0.1 * jax.random.normal(key_of[1], (D,), jnp.float32), 0.5, 1.5).astype(jnp.bfloat16)
    value_weight = normal_values(key_of[2], (D, KVH * HD), D ** -0.5, 0.0625, ((0, 128), (1, 2)))
    queries = draw_queries(jax.random.fold_in(key_of[8], 71), 0)
    keys = draw_keys(jax.random.fold_in(key_of[8], 71), 0)
    readout = normal_values(key_of[5], (QH * HD,), 0.25, 1.5, ((0, 2),), jnp.float32)
    targets = normal_values(key_of[6], (TOKENS,), 1.0, 4.0, ((0, 128),), jnp.float32)
    scored = touch_ends((jax.random.randint(key_of[7], (TOKENS,), 0, 4) < 3).astype(jnp.int32), jax.random.fold_in(key_of[7], 1), 0, 1)
    return {"hidden_states": hidden_states, "norm_gain": norm_gain, "value_weight": value_weight, "queries": queries, "keys": keys, "readout": readout, "targets": targets, "scored": scored}


EPS = 1e-06

def reference(hidden_states, norm_gain, value_weight, queries, keys, readout, targets, scored):
    count = TOKENS // TOK_DEV
    gain = norm_gain.astype(jnp.float32)
    read4 = readout.reshape(KVH, GROUP, HD)
    states_all = hidden_states.reshape(count, TOK_DEV, D)
    query_all = queries.reshape(count, TOK_DEV, QH * HD)
    key_all = keys.reshape(count, TOK_DEV, KVH * HD)
    target_all = targets.reshape(count, TOK_DEV)
    scored_all = scored.reshape(count, TOK_DEV)
    positions = jnp.arange(TOK_DEV)
    allowed = positions[None, :] <= positions[:, None]

    def sequence_pass(carry, items):
        grad_weight, grad_gain, grad_readout = carry
        states, query_s, key_s, target_s, scored_s = items
        xf = states.astype(jnp.float32)
        rms_inv = lax.rsqrt(lax.optimization_barrier(jnp.mean(xf * xf, axis=1, keepdims=True)) + EPS)
        normed = (xf * rms_inv * gain).astype(jnp.bfloat16)
        head_values = jnp.dot(normed, value_weight, preferred_element_type=jnp.float32).astype(jnp.bfloat16)
        q4 = query_s.reshape(TOK_DEV, KVH, GROUP, HD).astype(jnp.float32)
        k3 = key_s.reshape(TOK_DEV, KVH, HD).astype(jnp.float32)
        v3 = head_values.reshape(TOK_DEV, KVH, HD).astype(jnp.float32)
        scores = jnp.einsum('tkgd,skd->kgts', q4, k3) / math.sqrt(HD)
        scores = jnp.where(allowed, scores, -1e+30)
        top = lax.optimization_barrier(jnp.max(scores, axis=-1, keepdims=True))
        weights = jnp.exp(scores - top)
        probs = (weights / lax.optimization_barrier(jnp.sum(weights, axis=-1, keepdims=True))).astype(jnp.bfloat16)
        attended = jnp.einsum('kgts,skd->tkgd', probs.astype(jnp.float32), v3)
        values = lax.optimization_barrier(jnp.sum(attended * read4[None], axis=(1, 2, 3)))
        error = (values - target_s) * scored_s.astype(jnp.float32)
        grad_att = (error[:, None, None, None] * read4[None]).astype(jnp.bfloat16)
        grad_hv = jnp.einsum('kgts,tkgd->skd', probs.astype(jnp.float32), grad_att.astype(jnp.float32))
        grad_hv = grad_hv.astype(jnp.bfloat16).reshape(TOK_DEV, KVH * HD)
        grad_weight = grad_weight + lax.dot_general(normed, grad_hv, (((0,), (0,)), ((), ())), preferred_element_type=jnp.float32)
        grad_normed = lax.dot_general(grad_hv, value_weight, (((1,), (1,)), ((), ())), preferred_element_type=jnp.float32)
        grad_gain = grad_gain + lax.optimization_barrier(jnp.sum(grad_normed * xf * rms_inv, axis=0))
        grad_readout = grad_readout + lax.optimization_barrier(jnp.sum(error[:, None, None, None] * attended, axis=0)).reshape(QH * HD)
        scaled = grad_normed * gain
        total_dot = lax.optimization_barrier(jnp.sum(scaled * xf, axis=1, keepdims=True))
        log_scale = (rms_inv * total_dot)[:, 0]
        grad_input = (rms_inv * scaled - xf * rms_inv * rms_inv * rms_inv * total_dot / D).astype(jnp.bfloat16)
        return ((grad_weight, grad_gain, grad_readout), (values, grad_input, log_scale))
    start = (jnp.zeros((D, KVH * HD), jnp.float32), jnp.zeros((D,), jnp.float32), jnp.zeros((QH * HD,), jnp.float32))
    carry, outs = lax.scan(sequence_pass, start, (states_all, query_all, key_all, target_all, scored_all))
    grad_weight, grad_gain, grad_readout = carry
    values, grad_input, log_scale = outs
    return (values.reshape(TOKENS), grad_input.reshape(TOKENS, D), grad_weight, grad_gain, grad_readout, log_scale.reshape(TOKENS))
```

```python
import jax
import jax.numpy as jnp
from jax import lax
from jax.experimental import pallas as pl
from jax.experimental.pallas import tpu as pltpu
from jax.sharding import Mesh
from jax.sharding import PartitionSpec as P

HD = 128
GROUP = 8
EPS = 1e-06
F32 = jnp.float32
BF16 = jnp.bfloat16
HIGHEST = lax.Precision.HIGHEST
VMEM = pl.BlockSpec(memory_space=pltpu.VMEM)
PARAMS = pltpu.CompilerParams(vmem_limit_bytes=48 * 1024 * 1024)


def swap(v, axis, to):
    return lax.ppermute(v, axis, [(i, to(i)) for i in range(lax.axis_size(axis))])


def next_door(i):
    return i ^ 1


def two_off(i):
    return i ^ 2


def mirror_four(i):
    return 3 - i


def mirror_eight(i):
    return 7 - i


def cross(v):
    return lax.ppermute(v, ("yh", "yl"), [(0, 0), (1, 2), (2, 1), (3, 3)])


def split(bit, v, axis):
    n = v.shape[axis] // 2
    low = lax.slice_in_dim(v, 0, n, axis=axis)
    high = lax.slice_in_dim(v, n, 2 * n, axis=axis)
    return jnp.where(bit, high, low), jnp.where(bit, low, high)


def row_sum_of_transpose(a):
    return jnp.sum(a.T, axis=0, keepdims=True)


def probs_kernel(q_ref, k_ref, x_ref, p_ref, ss_ref, acc):
    step = pl.program_id(0)
    length = q_ref.shape[0]
    rows = lax.broadcasted_iota(jnp.int32, (length, length), 0)
    cols = lax.broadcasted_iota(jnp.int32, (length, length), 1)
    allowed = cols <= rows
    k = k_ref[...]
    for h in range(q_ref.shape[1] // HD):
        s = lax.dot_general(
            q_ref[:, h * HD : (h + 1) * HD], k, (((1,), (1,)), ((), ())), preferred_element_type=F32
        )
        s = jnp.where(allowed, s * (HD**-0.5), -1e30)
        e = jnp.exp(s - jnp.max(s, axis=1, keepdims=True))
        p_ref[h] = (e / jnp.sum(e, axis=1, keepdims=True)).astype(BF16)

    @pl.when(step == 0)
    def _():
        acc[...] = jnp.zeros_like(acc)

    total = acc[...]
    for b in range(x_ref.shape[1] // 128):
        xb = x_ref[:, b * 128 : (b + 1) * 128].astype(F32)
        total += xb * xb
    acc[...] = total

    @pl.when(step == pl.num_programs(0) - 1)
    def _():
        ss_ref[...] = row_sum_of_transpose(total)


def make_probs(queries, keys, x):
    length = queries.shape[0]
    heads = queries.shape[1] // HD
    steps = 4
    return pl.pallas_call(
        probs_kernel,
        grid=(steps,),
        in_specs=[
            pl.BlockSpec((length, heads // steps * HD), lambda i: (0, i)),
            pl.BlockSpec((length, HD), lambda i: (0, i // 2)),
            pl.BlockSpec((length, x.shape[1] // steps), lambda i: (0, i)),
        ],
        out_specs=[
            pl.BlockSpec((heads // steps, length, length), lambda i: (i, 0, 0)),
            pl.BlockSpec((1, length), lambda i: (0, 0)),
        ],
        out_shape=[
            jax.ShapeDtypeStruct((heads, length, length), BF16),
            jax.ShapeDtypeStruct((1, length), F32),
        ],
        scratch_shapes=[pltpu.VMEM((length, 128), F32)],
        compiler_params=PARAMS,
    )(queries, keys, x)


def project_kernel(blocks_ref, gain_ref, x_ref, vt_ref, gvt_ref, u_ref):
    low = lax.broadcasted_iota(jnp.int32, (16, 128), 1) < 64
    for b in range(blocks_ref.shape[0] // 2):
        one = blocks_ref[2 * b].astype(F32)
        two = blocks_ref[2 * b + 1].astype(F32)
        first = jnp.where(low, one, pltpu.roll(two, 64, 1))
        second = jnp.where(low, pltpu.roll(one, 64, 1), two)
        at = slice(b * 128, (b + 1) * 128)
        vt = jnp.concatenate([first, second], axis=0)
        vt_ref[:, at] = vt.astype(BF16)
        gvt_ref[:, at] = (vt * gain_ref[:, at].astype(F32)).astype(BF16)
    u_ref[...] = lax.dot_general(
        gvt_ref[...], x_ref[...], (((1,), (1,)), ((), ())), preferred_element_type=F32
    )


def project(blocks, gain, x):
    wide = x.shape[1]
    return pl.pallas_call(
        project_kernel,
        in_specs=[VMEM] * 3,
        out_specs=[VMEM] * 3,
        out_shape=[
            jax.ShapeDtypeStruct((32, wide), BF16),
            jax.ShapeDtypeStruct((32, wide), BF16),
            jax.ShapeDtypeStruct((32, x.shape[0]), F32),
        ],
        compiler_params=PARAMS,
    )(blocks, gain, x)


def values_kernel(width, p_ref, own_ref, got_ref, ss_ref, v_ref, u_ref, rms_ref):
    heads = p_ref.shape[0]
    got = got_ref[...]
    rms = lax.rsqrt((ss_ref[...] + got[heads : heads + 1]) / width + EPS)
    rms_ref[...] = rms
    u = own_ref[...] + got[:heads]
    u_ref[...] = u
    u = u * rms
    total = jnp.zeros(p_ref.shape[1:], F32)
    for j in range(heads):
        total += p_ref[j].astype(F32) * u[j : j + 1]
    v_ref[...] = row_sum_of_transpose(total)


def make_values(width, probs, own, got, ss):
    length = probs.shape[1]
    return pl.pallas_call(
        lambda *refs: values_kernel(width, *refs),
        in_specs=[VMEM] * 4,
        out_specs=[VMEM] * 3,
        out_shape=[
            jax.ShapeDtypeStruct((1, length), F32),
            jax.ShapeDtypeStruct(own.shape, F32),
            jax.ShapeDtypeStruct((1, length), F32),
        ],
        compiler_params=PARAMS,
    )(probs, own, got, ss)


def error_kernel(p_ref, u_ref, own_ref, got_ref, targets_ref, scored_ref, values_ref, c_ref):
    heads, length = u_ref.shape
    values = own_ref[...] + got_ref[...]
    values_ref[...] = values
    error = (values - targets_ref[...]) * scored_ref[...].astype(F32)
    spread = jnp.broadcast_to(error, (length, length)).T
    dot = jnp.zeros((1, length), F32)
    for j in range(heads):
        c = jnp.sum(p_ref[j].astype(F32) * spread, axis=0, keepdims=True)
        c_ref[j : j + 1] = c
        dot += c * u_ref[j : j + 1]
    c_ref[heads:] = jnp.broadcast_to(dot, (c_ref.shape[0] - heads, length))


def make_error(probs, u, own, got, targets, scored):
    length = probs.shape[1]
    return pl.pallas_call(
        error_kernel,
        in_specs=[VMEM] * 6,
        out_specs=[VMEM] * 2,
        out_shape=[
            jax.ShapeDtypeStruct((1, length), F32),
            jax.ShapeDtypeStruct((u.shape[0] + 8, length), F32),
        ],
        compiler_params=PARAMS,
    )(probs, u, own, got, targets, scored)


def weight_kernel(c_ref, rms_ref, gain_ref, vt_ref, x_ref, z_ref, part_ref):
    c = c_ref[...] * rms_ref[...]
    high = c.astype(BF16)
    low = (c - high.astype(F32)).astype(BF16)
    both = jnp.concatenate([high, low], axis=0)
    z = jnp.dot(both, x_ref[...], preferred_element_type=F32)
    z = z[:32] + z[32:]
    gain = gain_ref[...].astype(F32)
    part = jnp.sum(z * vt_ref[...].astype(F32), axis=0, keepdims=True)
    z = z * gain
    for b in range(z_ref.shape[0]):
        at = slice(b * 128, (b + 1) * 128)
        z_ref[b] = z[:, at]
        part_ref[b : b + 1] = part[:, at]


def weight_parts(c, rms, gain, vt, x):
    blocks = x.shape[1] // 128
    return pl.pallas_call(
        weight_kernel,
        in_specs=[VMEM] * 5,
        out_specs=[VMEM] * 2,
        out_shape=[
            jax.ShapeDtypeStruct((blocks, 32, 128), F32),
            jax.ShapeDtypeStruct((blocks, 128), F32),
        ],
        compiler_params=PARAMS,
    )(c, rms, gain, vt, x)


def input_kernel(width, c_ref, dot_ref, rms_ref, gvt_ref, x_ref, out_ref, log_ref):
    rms = rms_ref[...]
    length = rms.shape[1]
    c = c_ref[...] * rms
    high = c.astype(BF16)
    low = (c - high.astype(F32)).astype(BF16)
    log_scale = rms * dot_ref[...]
    log_ref[...] = log_scale
    back = jnp.broadcast_to(rms * rms * log_scale / width, (128, length)).T
    gvt = gvt_ref[...]
    grad = lax.dot_general(
        jnp.concatenate([high, low], axis=0),
        jnp.concatenate([gvt, gvt], axis=0),
        (((0,), (0,)), ((), ())),
        preferred_element_type=F32,
    )
    for b in range(grad.shape[1] // 128):
        at = slice(b * 128, (b + 1) * 128)
        out_ref[:, at] = (grad[:, at] - x_ref[:, at].astype(F32) * back).astype(BF16)


def input_grad(width, c, dot, rms, gvt, x):
    steps = 4
    length, wide = x.shape
    return pl.pallas_call(
        lambda *refs: input_kernel(width, *refs),
        grid=(steps,),
        in_specs=[
            pl.BlockSpec((32, length), lambda i: (0, 0)),
            pl.BlockSpec((1, length), lambda i: (0, 0)),
            pl.BlockSpec((1, length), lambda i: (0, 0)),
            pl.BlockSpec((32, wide // steps), lambda i: (0, i)),
            pl.BlockSpec((length, wide // steps), lambda i: (0, i)),
        ],
        out_specs=[
            pl.BlockSpec((length, wide // steps), lambda i: (0, i)),
            pl.BlockSpec((1, length), lambda i: (0, 0)),
        ],
        out_shape=[
            jax.ShapeDtypeStruct((length, wide), BF16),
            jax.ShapeDtypeStruct((1, length), F32),
        ],
        compiler_params=PARAMS,
    )(c, dot, rms, gvt, x)


def reduce_rows(z, part):
    zi = lax.axis_index("z")
    xi = lax.axis_index("x")
    core = lax.axis_index("core")

    def step(v, part, bit, axis, name, to):
        keep, send = split(bit, v, axis)
        n = send.size // 4096
        sent = jnp.concatenate([send.reshape(n, 32, 128), part[None]], axis=0)
        got = swap(sent, name, to)
        return keep + got[:n].reshape(keep.shape), part + got[n]

    z = z.reshape(4, 2, 4, 32, 128)
    z, part = step(z, part, core == 1, 1, "core", next_door)
    z, part = step(z, part, xi >= 2, 0, "x", mirror_four)
    z, part = step(z, part, xi % 2 == 1, 0, "x", next_door)
    z = z.reshape(4, 32, 128)
    z, part = step(z, part, zi >= 4, 0, "z", mirror_eight)
    z, part = step(z, part, zi % 4 >= 2, 0, "z", two_off)
    z = z[0]
    keep, send = split(zi % 2 == 1, z, 1)
    got = swap(jnp.concatenate([send, part.reshape(64, 64)], axis=0), "z", next_door)
    z = keep + got[:32]
    part = part.reshape(64, 64) + got[32:]
    keep, send = split(lax.axis_index("yh") == 1, z, 0)
    got = swap(jnp.concatenate([send, part], axis=0), "yh", next_door)
    z = cross(keep + got[:16])
    return z, (part + got[16:]).reshape(-1)


def all_reduce(v):
    v = v + swap(v, "core", next_door)
    v = v + swap(v, "x", next_door)
    v = v + swap(v, "x", mirror_four)
    v = v + swap(v, "z", next_door)
    v = v + swap(v, "z", two_off)
    v = v + swap(v, "z", mirror_eight)
    return v + swap(v, "yh", next_door)


def shards(hidden_states, norm_gain, value_weight, queries, keys, readout, targets, scored):
    x = hidden_states
    length = x.shape[0]
    width = x.shape[1] * 2
    yh = lax.axis_index("yh")
    yl = lax.axis_index("yl")
    gain = norm_gain[None]
    rows = value_weight.shape[0]
    w3 = value_weight.reshape(rows, 2, HD)
    r3 = readout.reshape(2, GROUP, HD)
    v = jnp.einsum("igd,gjd->gji", w3.astype(F32), r3, precision=HIGHEST)
    v = v.reshape(2 * GROUP, rows).astype(BF16)

    probs, ss = make_probs(queries, keys, x)

    v = cross(v)
    other = swap(v, "yh", next_door)
    v = jnp.concatenate([jnp.where(yh == 0, v, other), jnp.where(yh == 0, other, v)], axis=1)
    blocks = lax.all_to_all(
        jnp.broadcast_to(v, (64,) + v.shape), ("x", "core", "z"), 0, 0
    )
    vt, gvt, u = project(blocks, gain, x)
    own, send = split(yl == 1, u, 0)
    got = swap(jnp.concatenate([send, jnp.broadcast_to(ss, (8, length))], axis=0), "yl", next_door)
    part_values, u, rms = make_values(width, probs, own, got, ss)
    got = swap(part_values, "yl", next_door)
    values, c = make_error(probs, u, part_values, got, targets[None], scored[None])
    got = swap(c, "yl", next_door)
    dot = c[16:17] + got[16:17]
    c = jnp.concatenate([jnp.where(yl == 0, c[:16], got[:16]), jnp.where(yl == 0, got[:16], c[:16])], axis=0)
    z, part = weight_parts(c, rms, gain, vt, x)
    grad_input, log_scale = input_grad(width, c, dot, rms, gvt, x)
    z, grad_gain = reduce_rows(z, part)
    z3 = z.reshape(2, GROUP, rows)
    grad_weight = jnp.einsum("gji,gjd->igd", z3, r3, precision=HIGHEST).reshape(rows, 2 * HD)
    read_part = jnp.einsum("gji,igd->gjd", z3, w3.astype(F32), precision=HIGHEST)
    grad_readout = all_reduce(read_part.reshape(16, HD)).reshape(-1)
    return (values[0], grad_input, grad_weight, grad_gain, grad_readout, log_scale[0])


def solution(mesh):
    fine = Mesh(mesh.devices.reshape(2, 4, 2, 8, 2), ("yh", "x", "core", "z", "yl"))
    seq = ("yh", "x", "core", "z")
    return jax.shard_map(
        shards,
        mesh=fine,
        in_specs=(
            P(seq, "yl"),
            P("yl"),
            P(seq, "yl"),
            P(seq, "yl"),
            P(seq, "yl"),
            P("yl"),
            P(seq),
            P(seq),
        ),
        out_specs=(
            P(seq),
            P(seq, "yl"),
            P(seq, "yl"),
            P("yl"),
            P("yl"),
            P(seq),
        ),
        check_vma=False,
    )
```

```python
import jax
import jax.numpy as jnp
from jax import lax
from jax.experimental import pallas as pl
from jax.experimental.pallas import tpu as pltpu
from jax.sharding import Mesh
from jax.sharding import PartitionSpec as P

HD = 128
GROUP = 8
EPS = 1e-06
F32 = jnp.float32
BF16 = jnp.bfloat16
HIGHEST = lax.Precision.HIGHEST
VMEM = pl.BlockSpec(memory_space=pltpu.VMEM)
PARAMS = pltpu.CompilerParams(vmem_limit_bytes=48 * 1024 * 1024)


SEQ = ("yh", "x", "core", "z")
ROWS = 64
BLOCKS = 64
HALF = 16


def swap(v, axis):
    return lax.ppermute(v, axis, [(0, 1), (1, 0)])


def cross(v):
    return lax.ppermute(v, ("yh", "yl"), [(0, 0), (1, 2), (2, 1), (3, 3)])


def split(bit, v, axis):
    n = v.shape[axis] // 2
    low = lax.slice_in_dim(v, 0, n, axis=axis)
    high = lax.slice_in_dim(v, n, 2 * n, axis=axis)
    return jnp.where(bit, high, low), jnp.where(bit, low, high)


def whole(body, out_shape, *args):
    many = isinstance(out_shape, list)
    return pl.pallas_call(
        body,
        in_specs=[VMEM] * len(args),
        out_specs=[VMEM] * len(out_shape) if many else VMEM,
        out_shape=out_shape,
        compiler_params=PARAMS,
    )(*args)


def shape(*dims, dtype=F32):
    return jax.ShapeDtypeStruct(dims, dtype)


def exact_dot(a, b, dims):
    return lax.dot_general(a, b, (dims, ((), ())), precision=HIGHEST, preferred_element_type=F32)


def left_lanes(rows):
    return lax.broadcasted_iota(jnp.int32, (rows, 128), 1) < 64


def read_kernel(w_ref, r_ref, v_ref):
    parts = []
    for g in range(2):
        w = w_ref[:, g * HD : (g + 1) * HD].astype(F32)
        parts.append(exact_dot(r_ref[g * GROUP : (g + 1) * GROUP], w, ((1,), (1,))))
    v_ref[...] = jnp.concatenate(parts, axis=1).astype(BF16)


def row_sum_of_transpose(a):
    return jnp.sum(a.T, axis=0, keepdims=True)


def probs_kernel(q_ref, k_ref, x_ref, p_ref, ss_ref, acc):
    step = pl.program_id(0)
    length = q_ref.shape[0]
    rows = lax.broadcasted_iota(jnp.int32, (length, length), 0)
    cols = lax.broadcasted_iota(jnp.int32, (length, length), 1)
    allowed = cols <= rows
    k = k_ref[...]
    for h in range(q_ref.shape[1] // HD):
        s = lax.dot_general(
            q_ref[:, h * HD : (h + 1) * HD], k, (((1,), (1,)), ((), ())), preferred_element_type=F32
        )
        s = jnp.where(allowed, s * (HD**-0.5), -1e30)
        e = jnp.exp(s - jnp.max(s, axis=1, keepdims=True))
        p_ref[h] = (e / jnp.sum(e, axis=1, keepdims=True)).astype(BF16)

    @pl.when(step == 0)
    def _():
        acc[...] = jnp.zeros_like(acc)

    total = acc[...]
    for b in range(x_ref.shape[1] // 128):
        xb = x_ref[:, b * 128 : (b + 1) * 128].astype(F32)
        total += xb * xb
    acc[...] = total

    @pl.when(step == pl.num_programs(0) - 1)
    def _():
        ss_ref[...] = row_sum_of_transpose(total)


def make_probs(queries, keys, x):
    length = queries.shape[0]
    heads = queries.shape[1] // HD
    steps = 4
    return pl.pallas_call(
        probs_kernel,
        grid=(steps,),
        in_specs=[
            pl.BlockSpec((length, heads // steps * HD), lambda i: (0, i)),
            pl.BlockSpec((length, HD), lambda i: (0, i // 2)),
            pl.BlockSpec((length, x.shape[1] // steps), lambda i: (0, i)),
        ],
        out_specs=[
            pl.BlockSpec((heads // steps, length, length), lambda i: (i, 0, 0)),
            pl.BlockSpec((1, length), lambda i: (0, 0)),
        ],
        out_shape=[
            jax.ShapeDtypeStruct((heads, length, length), BF16),
            jax.ShapeDtypeStruct((1, length), F32),
        ],
        scratch_shapes=[pltpu.VMEM((length, 128), F32)],
        compiler_params=PARAMS,
    )(queries, keys, x)


def project_kernel(blocks_ref, gain_ref, x_ref, gvt_ref, u_ref):
    low = left_lanes(8)
    for b in range(BLOCKS // 2):
        at = slice(b * 128, (b + 1) * 128)
        heads = []
        for h in range(2):
            row = (h * BLOCKS + 2 * b) * 8
            pair = blocks_ref[row : row + 16].astype(F32)
            one, two = pair[:8], pair[8:]
            heads.append(jnp.where(low, one, pltpu.roll(two, 64, 1)))
            heads.append(jnp.where(low, pltpu.roll(one, 64, 1), two))
        vt = jnp.concatenate(heads, axis=0)
        gvt_ref[:, at] = (vt * gain_ref[:, at].astype(F32)).astype(BF16)
    u_ref[...] = lax.dot_general(
        gvt_ref[...], x_ref[...], (((1,), (1,)), ((), ())), preferred_element_type=F32
    )


def project(blocks, gain, x):
    length, wide = x.shape
    return whole(project_kernel, [shape(32, wide, dtype=BF16), shape(32, length)], blocks, gain, x)


def values_kernel(width, p_ref, own_ref, got_ref, ss_ref, v_ref, u_ref, rms_ref):
    heads = p_ref.shape[0]
    got = got_ref[...]
    rms = lax.rsqrt((ss_ref[...] + got[heads : heads + 1]) / width + EPS)
    rms_ref[...] = rms
    u = own_ref[...] + got[:heads]
    u_ref[...] = u
    u = u * rms
    total = jnp.zeros(p_ref.shape[1:], F32)
    for j in range(heads):
        total += p_ref[j].astype(F32) * u[j : j + 1]
    v_ref[...] = row_sum_of_transpose(total)


def make_values(width, probs, own, got, ss):
    length = probs.shape[1]
    return pl.pallas_call(
        lambda *refs: values_kernel(width, *refs),
        in_specs=[VMEM] * 4,
        out_specs=[VMEM] * 3,
        out_shape=[
            jax.ShapeDtypeStruct((1, length), F32),
            jax.ShapeDtypeStruct(own.shape, F32),
            jax.ShapeDtypeStruct((1, length), F32),
        ],
        compiler_params=PARAMS,
    )(probs, own, got, ss)


def error_kernel(p_ref, u_ref, own_ref, got_ref, targets_ref, scored_ref, values_ref, c_ref):
    heads, length = u_ref.shape
    values = own_ref[...] + got_ref[...]
    values_ref[...] = values
    error = (values - targets_ref[...]) * scored_ref[...].astype(F32)
    spread = jnp.broadcast_to(error, (length, length)).T
    dot = jnp.zeros((1, length), F32)
    for j in range(heads):
        c = jnp.sum(p_ref[j].astype(F32) * spread, axis=0, keepdims=True)
        c_ref[j : j + 1] = c
        dot += c * u_ref[j : j + 1]
    c_ref[heads:] = jnp.broadcast_to(dot, (c_ref.shape[0] - heads, length))


def make_error(probs, u, own, got, targets, scored):
    length = probs.shape[1]
    return pl.pallas_call(
        error_kernel,
        in_specs=[VMEM] * 6,
        out_specs=[VMEM] * 2,
        out_shape=[
            jax.ShapeDtypeStruct((1, length), F32),
            jax.ShapeDtypeStruct((u.shape[0] + 8, length), F32),
        ],
        compiler_params=PARAMS,
    )(probs, u, own, got, targets, scored)


def weight_kernel(c_ref, rms_ref, x_ref, z_ref):
    c = c_ref[...] * rms_ref[...]
    high = c.astype(BF16)
    low = (c - high.astype(F32)).astype(BF16)
    both = jnp.concatenate([high, low], axis=0)
    z = jnp.dot(both, x_ref[...], preferred_element_type=F32)
    z = z[:32] + z[32:]
    left = left_lanes(8)
    for b in range(BLOCKS // 2):
        for h in range(2):
            one = z[h * HALF : h * HALF + 8, b * 128 : (b + 1) * 128]
            two = z[h * HALF + 8 : h * HALF + 16, b * 128 : (b + 1) * 128]
            first = jnp.where(left, one, pltpu.roll(two, 64, 1))
            second = jnp.where(left, pltpu.roll(one, 64, 1), two)
            row = (h * BLOCKS + 2 * b) * 8
            z_ref[row : row + 16] = jnp.concatenate([first, second], axis=0).astype(BF16)


def sum_kernel(parts_ref, gain_ref, v_ref, z_ref, part_ref):
    total = jnp.zeros((8, 128), F32)
    for b in range(parts_ref.shape[0] // 16):
        pair = parts_ref[b * 16 : (b + 1) * 16].astype(F32)
        total += pair[:8] + pair[8:]
    z_ref[...] = total * gain_ref[...].astype(F32)
    part = jnp.sum(total * v_ref[...].astype(F32), axis=0, keepdims=True)
    part_ref[...] = jnp.broadcast_to(part + pltpu.roll(part, 64, 1), (8, 128))


def outputs_kernel(z_ref, w_ref, r_ref, part_ref, grad_ref, read_ref):
    for g in range(2):
        z = z_ref[:, g * ROWS : (g + 1) * ROWS]
        at = slice(g * HD, (g + 1) * HD)
        heads = slice(g * GROUP, (g + 1) * GROUP)
        grad_ref[:, at] = exact_dot(z, r_ref[heads], ((0,), (0,)))
        read_ref[heads] = exact_dot(z, w_ref[:, at].astype(F32), ((1,), (0,)))
    read_ref[HALF:] = part_ref[...]


def last_kernel(all_ref, read_ref, gain_ref):
    left = left_lanes(1)
    total = all_ref[0].astype(F32)
    for i in range(1, 64):
        total += all_ref[i].astype(F32)
    read_ref[...] = total[:HALF]
    for xi in range(4):
        for zp in range(4):
            i = xi * 8 + 2 * zp
            one = all_ref[i].astype(F32) + all_ref[32 + i].astype(F32)
            two = all_ref[i + 1].astype(F32) + all_ref[33 + i].astype(F32)
            one, two = one[HALF : HALF + 1], two[HALF : HALF + 1]
            row = xi * 8 + zp
            gain_ref[row : row + 1] = jnp.where(left, one, pltpu.roll(two, 64, 1))
            gain_ref[row + 4 : row + 5] = jnp.where(left, pltpu.roll(one, 64, 1), two)


def input_kernel(width, c_ref, dot_ref, rms_ref, gvt_ref, x_ref, out_ref, log_ref):
    rms = rms_ref[...]
    length = rms.shape[1]
    c = c_ref[...] * rms
    high = c.astype(BF16)
    low = (c - high.astype(F32)).astype(BF16)
    log_scale = rms * dot_ref[...]
    log_ref[...] = log_scale
    back = jnp.broadcast_to(rms * rms * log_scale / width, (128, length)).T
    gvt = gvt_ref[...]
    grad = lax.dot_general(
        jnp.concatenate([high, low], axis=0),
        jnp.concatenate([gvt, gvt], axis=0),
        (((0,), (0,)), ((), ())),
        preferred_element_type=F32,
    )
    for b in range(grad.shape[1] // 128):
        at = slice(b * 128, (b + 1) * 128)
        out_ref[:, at] = (grad[:, at] - x_ref[:, at].astype(F32) * back).astype(BF16)


def input_grad(width, c, dot, rms, gvt, x):
    steps = 4
    length, wide = x.shape
    return pl.pallas_call(
        lambda *refs: input_kernel(width, *refs),
        grid=(steps,),
        in_specs=[
            pl.BlockSpec((32, length), lambda i: (0, 0)),
            pl.BlockSpec((1, length), lambda i: (0, 0)),
            pl.BlockSpec((1, length), lambda i: (0, 0)),
            pl.BlockSpec((32, wide // steps), lambda i: (0, i)),
            pl.BlockSpec((length, wide // steps), lambda i: (0, i)),
        ],
        out_specs=[
            pl.BlockSpec((length, wide // steps), lambda i: (0, i)),
            pl.BlockSpec((1, length), lambda i: (0, 0)),
        ],
        out_shape=[
            jax.ShapeDtypeStruct((length, wide), BF16),
            jax.ShapeDtypeStruct((1, length), F32),
        ],
        compiler_params=PARAMS,
    )(c, dot, rms, gvt, x)


def shards(hidden_states, norm_gain, value_weight, queries, keys, readout, targets, scored):
    x = hidden_states
    length = x.shape[0]
    width = x.shape[1] * 2
    yl = lax.axis_index("yl")
    core = lax.axis_index("core")
    gain = norm_gain[None]
    rows = value_weight.shape[0]
    read = readout.reshape(HALF, HD)
    v = cross(whole(read_kernel, shape(8, 128, dtype=BF16), value_weight, read))
    blocks = lax.all_to_all(jnp.broadcast_to(v, (128, 8, 128)), SEQ, 0, 0)
    probs, ss = make_probs(queries, keys, x)
    gvt, u = project(blocks.reshape(1024, 128), gain, x)
    own, send = split(yl == 1, u, 0)
    got = swap(jnp.concatenate([send, jnp.broadcast_to(ss, (8, length))], axis=0), "yl")
    part_values, u, rms = make_values(width, probs, own, got, ss)
    got = swap(part_values, "yl")
    values, c = make_error(probs, u, part_values, got, targets[None], scored[None])
    got = swap(c, "yl")
    dot = c[16:17] + got[16:17]
    c = jnp.concatenate([jnp.where(yl == 0, c[:16], got[:16]), jnp.where(yl == 0, got[:16], c[:16])], axis=0)
    z = whole(weight_kernel, shape(1024, 128, dtype=BF16), c, rms, x)
    z = lax.all_to_all(z.reshape(128, 8, 128), SEQ, 0, 0).reshape(1024, 128)
    grad_input, log_scale = input_grad(width, c, dot, rms, gvt, x)
    at = (lax.axis_index("x") * 2 + core) * 8 + lax.axis_index("z")
    own_gain = lax.dynamic_slice(norm_gain, (at * rows,), (rows,))
    own_gain = jnp.concatenate([own_gain, own_gain])[None]
    z, part = whole(sum_kernel, [shape(8, 128), shape(8, 128)], z, own_gain, v)
    grad_weight, tail = whole(
        outputs_kernel, [shape(rows, 2 * HD), shape(HALF + 8, 128)], cross(z), value_weight, read, part
    )
    got = swap(tail, "core")
    pair = jnp.where((jnp.arange(128) < 64) == (core == 0), tail[HALF:], got[HALF:])
    tail = jnp.concatenate([tail[:HALF] + got[:HALF], pair], axis=0).astype(BF16)
    tails = lax.all_to_all(jnp.broadcast_to(tail, (64,) + tail.shape), ("yh", "x", "z"), 0, 0)
    grad_readout, grad_gain = whole(last_kernel, [shape(HALF, HD), shape(32, 128)], tails)
    return (values[0], grad_input, grad_weight, grad_gain.reshape(-1), grad_readout.reshape(-1), log_scale[0])


def solution(mesh):
    fine = Mesh(mesh.devices.reshape(2, 4, 2, 8, 2), ("yh", "x", "core", "z", "yl"))
    seq = ("yh", "x", "core", "z")
    return jax.shard_map(
        shards,
        mesh=fine,
        in_specs=(
            P(seq, "yl"),
            P("yl"),
            P(seq, "yl"),
            P(seq, "yl"),
            P(seq, "yl"),
            P("yl"),
            P(seq),
            P(seq),
        ),
        out_specs=(
            P(seq),
            P(seq, "yl"),
            P(seq, "yl"),
            P("yl"),
            P("yl"),
            P(seq),
        ),
        check_vma=False,
    )
```

```python
import jax
import jax.numpy as jnp
from jax import lax
from jax.experimental import pallas as pl
from jax.experimental.pallas import tpu as pltpu
from jax.sharding import Mesh
from jax.sharding import PartitionSpec as P

HD = 128
GROUP = 8
EPS = 1e-06
F32 = jnp.float32
BF16 = jnp.bfloat16
HIGHEST = lax.Precision.HIGHEST
VMEM = pl.BlockSpec(memory_space=pltpu.VMEM)
HBM = pl.BlockSpec(memory_space=pltpu.HBM)
ANY = pl.BlockSpec(memory_space=pl.ANY)
PARAMS = pltpu.CompilerParams(vmem_limit_bytes=16 * 1024 * 1024)


FAR = ("yh", "x", "z")
PLANE = ("x", "z")
NEAR = ("yh", "core", "yl")
ROWS = 64
BLOCKS = 64
HALF = 16


def swap(v, axis):
    return lax.ppermute(v, axis, [(0, 1), (1, 0)])


def cross(v):
    return lax.ppermute(v, ("yh", "yl"), [(0, 0), (1, 2), (2, 1), (3, 3)])


def split(bit, v, axis):
    n = v.shape[axis] // 2
    low = lax.slice_in_dim(v, 0, n, axis=axis)
    high = lax.slice_in_dim(v, n, 2 * n, axis=axis)
    return jnp.where(bit, high, low), jnp.where(bit, low, high)


def whole(body, out_shape, *args, scratch=()):
    many = isinstance(out_shape, list)
    return pl.pallas_call(
        body,
        in_specs=[VMEM] * len(args),
        out_specs=[VMEM] * len(out_shape) if many else VMEM,
        out_shape=out_shape,
        scratch_shapes=scratch,
        compiler_params=PARAMS,
    )(*args)


def shape(*dims, dtype=F32):
    return jax.ShapeDtypeStruct(dims, dtype)


def exact_dot(a, b, dims):
    return lax.dot_general(a, b, (dims, ((), ())), precision=HIGHEST, preferred_element_type=F32)


def left_lanes(rows):
    return lax.broadcasted_iota(jnp.int32, (rows, 128), 1) < 64


def read_kernel(w_ref, r_ref, v_ref, wv_ref, rv_ref, sems):
    copies = [
        pltpu.make_async_copy(w_ref, wv_ref, sems.at[0]),
        pltpu.make_async_copy(r_ref, rv_ref, sems.at[1]),
    ]
    for copy in copies:
        copy.start()
    for copy in copies:
        copy.wait()
    parts = []
    for g in range(2):
        w = wv_ref[:, g * HD : (g + 1) * HD].astype(F32)
        parts.append(exact_dot(rv_ref[g * GROUP : (g + 1) * GROUP], w, ((1,), (1,))))
    v = jnp.concatenate(parts, axis=1)
    v = jnp.concatenate([v, v], axis=0).astype(BF16)
    for i in range(32):
        v_ref[i * 16 : (i + 1) * 16] = v


def read_weight(w, read):
    return pl.pallas_call(
        read_kernel,
        in_specs=[HBM] * 2,
        out_specs=VMEM,
        out_shape=shape(512, 128, dtype=BF16),
        scratch_shapes=[
            pltpu.VMEM(w.shape, BF16), pltpu.VMEM(read.shape, F32), pltpu.SemaphoreType.DMA((2,))
        ],
        compiler_params=PARAMS,
    )(w, read)


def row_sum_of_transpose(a):
    return jnp.sum(a.T, axis=0, keepdims=True)


def attention(q_ref, k_ref, p_ref):
    length = q_ref.shape[0]
    rows = lax.broadcasted_iota(jnp.int32, (length, length), 0)
    cols = lax.broadcasted_iota(jnp.int32, (length, length), 1)
    allowed = cols <= rows
    for h in range(HALF):
        g = h // GROUP
        s = lax.dot_general(
            q_ref[:, h * HD : (h + 1) * HD],
            k_ref[:, g * HD : (g + 1) * HD],
            (((1,), (1,)), ((), ())),
            preferred_element_type=F32,
        )
        s = jnp.where(allowed, s * (HD**-0.5), -1e30)
        e = jnp.exp(s - jnp.max(s, axis=1, keepdims=True))
        p_ref[h] = (e / jnp.sum(e, axis=1, keepdims=True)).astype(BF16)


def early_kernel(x_ref, q_ref, k_ref, after_ref, xv_ref, p_ref, ss_ref, qv_ref, kv_ref, sems):
    copies = [
        pltpu.make_async_copy(q_ref, qv_ref, sems.at[0]),
        pltpu.make_async_copy(k_ref, kv_ref, sems.at[1]),
        pltpu.make_async_copy(x_ref, xv_ref, sems.at[2]),
    ]
    for copy in copies:
        copy.start()
    copies[0].wait()
    copies[1].wait()
    attention(qv_ref, kv_ref, p_ref)
    copies[2].wait()
    total = jnp.zeros((xv_ref.shape[0], 128), F32)
    for b in range(xv_ref.shape[1] // 128):
        xb = xv_ref[:, b * 128 : (b + 1) * 128].astype(F32)
        total += xb * xb
    ss_ref[...] = row_sum_of_transpose(total)


def early(x, queries, keys, after):
    length = x.shape[0]
    return pl.pallas_call(
        early_kernel,
        in_specs=[HBM] * 3 + [ANY],
        out_specs=[VMEM] * 3,
        out_shape=[shape(*x.shape, dtype=BF16), shape(HALF, length, length, dtype=BF16), shape(1, length)],
        scratch_shapes=[
            pltpu.VMEM(queries.shape, BF16), pltpu.VMEM(keys.shape, BF16), pltpu.SemaphoreType.DMA((3,))
        ],
        compiler_params=PARAMS,
    )(x, queries, keys, after)


def project_kernel(
    own_ref, own_y_ref, got_ref, got_y_ref, gain_ref, x_ref, ss_ref, gvt_ref, u_ref, send_ref
):
    core = lax.axis_index("core")
    low = left_lanes(8)
    for b in range(BLOCKS // 2):
        xi, c, zp = b // 8, b // 4 % 2, b % 4
        at = slice(b * 128, (b + 1) * 128)
        row = (xi * 8 + 2 * zp) * 8
        halves = []
        for here, there in ((own_ref, got_ref), (own_y_ref, got_y_ref)):
            pair = jnp.where(
                core == c, here[row : row + 16].astype(F32), there[row : row + 16].astype(F32)
            )
            one, two = pair[:8], pair[8:]
            halves.append(jnp.where(low, one, pltpu.roll(two, 64, 1)))
            halves.append(jnp.where(low, pltpu.roll(one, 64, 1), two))
        vt = jnp.concatenate(halves, axis=0)
        gvt_ref[:, at] = (vt * gain_ref[:, at].astype(F32)).astype(BF16)
    u = lax.dot_general(
        gvt_ref[...], x_ref[...], (((1,), (1,)), ((), ())), preferred_element_type=F32
    )
    u_ref[...] = u[:HALF]
    send_ref[:HALF] = u[HALF:]
    send_ref[HALF:] = jnp.broadcast_to(ss_ref[...], (8, u.shape[1]))


def project(vs, gain, x, ss):
    length, wide = x.shape
    return whole(
        project_kernel,
        [shape(32, wide, dtype=BF16), shape(HALF, length), shape(HALF + 8, length)],
        *vs, gain, x, ss,
    )


def values_kernel(width, p_ref, own_ref, got_ref, ss_ref, v_ref, u_ref, rms_ref):
    got = got_ref[...]
    rms = lax.rsqrt((ss_ref[...] + got[HALF : HALF + 1]) / width + EPS)
    rms_ref[...] = rms
    u = own_ref[...] + got[:HALF]
    u_ref[...] = u
    u = u * rms
    total = jnp.zeros(p_ref.shape[1:], F32)
    for j in range(HALF):
        total += p_ref[j].astype(F32) * u[j : j + 1]
    v_ref[...] = row_sum_of_transpose(total)


def make_values(width, probs, own, got, ss):
    length = probs.shape[1]
    return whole(
        lambda *refs: values_kernel(width, *refs),
        [shape(1, length), shape(HALF, length), shape(1, length)],
        probs, own, got, ss,
    )


def error_kernel(p_ref, u_ref, own_ref, got_ref, targets_ref, scored_ref, values_ref, c_ref):
    length = u_ref.shape[1]
    values = own_ref[...] + got_ref[...]
    values_ref[...] = values
    error = (values - targets_ref[...]) * scored_ref[...].astype(F32)
    spread = jnp.broadcast_to(error, (length, length)).T
    rows = [jnp.sum(p_ref[j].astype(F32) * spread, axis=0, keepdims=True) for j in range(HALF)]
    c = jnp.concatenate(rows, axis=0)
    c_ref[:HALF] = c
    c_ref[HALF:] = jnp.broadcast_to(jnp.sum(c * u_ref[...], axis=0, keepdims=True), (8, length))


def make_error(probs, u, own, got, targets, scored):
    length = probs.shape[1]
    return whole(
        error_kernel, [shape(1, length), shape(HALF + 8, length)], probs, u, own, got, targets, scored
    )


def rows_kernel(own_ref, got_ref, rms_ref, x_ref, c_ref, dot_ref, keep_ref, send_ref):
    core = lax.axis_index("core")
    c = jnp.concatenate([own_ref[:HALF], got_ref[:HALF]], axis=0) * rms_ref[...]
    c_ref[...] = c
    dot_ref[...] = own_ref[HALF : HALF + 1] + got_ref[HALF : HALF + 1]
    high = c.astype(BF16)
    low = (c - high.astype(F32)).astype(BF16)
    both = jnp.concatenate([high, low], axis=0)
    z = jnp.dot(both, x_ref[...], preferred_element_type=F32)
    z = z[:32] + z[32:]
    left = left_lanes(8)

    def chunks(b):
        at = slice(b * 128, (b + 1) * 128)
        parts = [z[i * 8 : (i + 1) * 8, at] for i in range(4)]
        even = [jnp.where(left, parts[i], pltpu.roll(parts[i + 1], 64, 1)) for i in (0, 2)]
        odd = [jnp.where(left, pltpu.roll(parts[i], 64, 1), parts[i + 1]) for i in (0, 2)]
        return jnp.concatenate([*even, *odd], axis=0)

    for xi in range(4):
        for zp in range(4):
            at = pl.ds((xi * 4 + zp) * 32, 32)
            zero, one = chunks(xi * 8 + zp), chunks(xi * 8 + 4 + zp)
            keep_ref[at] = jnp.where(core == 0, zero, one)
            send_ref[at] = jnp.where(core == 0, one, zero)


def make_rows(own, got, rms, x):
    length = x.shape[0]
    return whole(
        rows_kernel,
        [shape(32, length), shape(1, length), shape(512, 128), shape(512, 128)],
        own, got, rms, x,
    )


def pick_kernel(v_ref, own_ref, send_ref):
    side = lax.axis_index("yl")
    own_ref[...] = v_ref[pl.ds(pl.multiple_of(side * 256, 256), 256)]
    send_ref[...] = v_ref[pl.ds(pl.multiple_of((1 - side) * 256, 256), 256)]


def sum_kernel(parts_ref, gain_ref, own_ref, own_y_ref, w_ref, w_other_ref, tails_ref):
    side = lax.axis_index("yl")
    straight = lax.axis_index("yh") == side
    xi, zi = lax.axis_index("x"), lax.axis_index("z")
    even = zi % 2 == 0
    at = pl.ds(pl.multiple_of((xi * 4 + zi // 2) * 16, 16), 16)
    vs = []
    for ref in (own_ref, own_y_ref):
        pair = ref[at].astype(F32)
        vs.append(jnp.where(even, pair[:8], pair[8:]))
    v = jnp.concatenate(vs, axis=0)
    spot = (xi * 2 + lax.axis_index("core")) * 4 + zi // 2
    gain = jnp.zeros((1, 128), F32)
    for b in range(BLOCKS // 2):
        gain = jnp.where(spot == b, gain_ref[:, b * 128 : (b + 1) * 128].astype(F32), gain)
    gain = jnp.where(left_lanes(1) == even, gain, pltpu.roll(gain, 64, 1))
    total = jnp.zeros((HALF, 128), F32)
    for b in range(32):
        total += parts_ref[b].astype(F32)
    z = total * gain
    part = jnp.sum(total * v, axis=0, keepdims=True)
    part = jnp.broadcast_to(part + pltpu.roll(part, 64, 1), (8, 128))
    w, w_other = w_ref[...].astype(F32), w_other_ref[...].astype(F32)
    tails = []
    for h, weight in enumerate((jnp.where(straight, w, w_other), jnp.where(straight, w_other, w))):
        rows = z[h * 8 : (h + 1) * 8]
        reads = [
            exact_dot(rows[:, g * ROWS : (g + 1) * ROWS], weight[:, g * HD : (g + 1) * HD], ((1,), (0,)))
            for g in range(2)
        ]
        tails.append(jnp.concatenate([*reads, part, rows], axis=0))
    for i in range(8):
        tails_ref[i] = jnp.where(side == i % 2, tails[0], tails[1])


def weight_kernel(z_ref, r_ref, grad_ref):
    for g in range(2):
        z = z_ref[:, g * ROWS : (g + 1) * ROWS]
        grad_ref[:, g * HD : (g + 1) * HD] = exact_dot(z, r_ref[g * GROUP : (g + 1) * GROUP], ((0,), (0,)))


def near_kernel(tails_ref, out_ref, z_ref):
    core, side, far = lax.axis_index("core"), lax.axis_index("yl"), lax.axis_index("yh")
    read = tails_ref[0][:HALF]
    for i in range(1, 8):
        read += tails_ref[i][:HALF]
    gain = slice(HALF, HALF + 8)
    zero = tails_ref[side][gain] + tails_ref[4 + side][gain]
    one = tails_ref[2 + side][gain] + tails_ref[6 + side][gain]
    at = 2 * core + far
    z_ref[...] = tails_ref[at][HALF + 8 :] + tails_ref[4 + at][HALF + 8 :]
    tail = jnp.concatenate([read, jnp.where(left_lanes(8), zero, one)], axis=0).astype(BF16)
    for i in range(32):
        out_ref[i] = tail


def last_kernel(all_ref, read_ref, gain_ref):
    left = left_lanes(1)
    total = all_ref[0].astype(F32)
    for i in range(1, 32):
        total += all_ref[i].astype(F32)
    read_ref[...] = total[:HALF]
    for xi in range(4):
        for zp in range(4):
            i = xi * 8 + 2 * zp
            one = all_ref[i].astype(F32)[HALF : HALF + 1]
            two = all_ref[i + 1].astype(F32)[HALF : HALF + 1]
            row = xi * 8 + zp
            gain_ref[row : row + 1] = jnp.where(left, one, pltpu.roll(two, 64, 1))
            gain_ref[row + 4 : row + 5] = jnp.where(left, pltpu.roll(one, 64, 1), two)


def input_kernel(width, c_ref, dot_ref, rms_ref, gvt_ref, x_ref, after_ref, out_ref, log_ref):
    rms = rms_ref[...]
    length = rms.shape[1]
    c = c_ref[...]
    high = c.astype(BF16)
    low = (c - high.astype(F32)).astype(BF16)
    log_scale = rms * dot_ref[...]
    log_ref[...] = log_scale
    back = jnp.broadcast_to(rms * rms * log_scale / width, (128, length)).T
    gvt = gvt_ref[...]
    grad = lax.dot_general(
        jnp.concatenate([high, low], axis=0),
        jnp.concatenate([gvt, gvt], axis=0),
        (((0,), (0,)), ((), ())),
        preferred_element_type=F32,
    )
    for b in range(grad.shape[1] // 128):
        at = slice(b * 128, (b + 1) * 128)
        out_ref[:, at] = (grad[:, at] - x_ref[:, at].astype(F32) * back).astype(BF16)


def input_grad(width, c, dot, rms, gvt, x, after):
    steps = 4
    length, wide = x.shape
    return pl.pallas_call(
        lambda *refs: input_kernel(width, *refs),
        grid=(steps,),
        in_specs=[
            pl.BlockSpec((32, length), lambda i: (0, 0)),
            pl.BlockSpec((1, length), lambda i: (0, 0)),
            pl.BlockSpec((1, length), lambda i: (0, 0)),
            pl.BlockSpec((32, wide // steps), lambda i: (0, i)),
            pl.BlockSpec((length, wide // steps), lambda i: (0, i)),
            ANY,
        ],
        out_specs=[
            pl.BlockSpec((length, wide // steps), lambda i: (0, i)),
            pl.BlockSpec((1, length), lambda i: (0, 0)),
        ],
        out_shape=[shape(length, wide, dtype=BF16), shape(1, length)],
        compiler_params=PARAMS,
    )(c, dot, rms, gvt, x, after)


def together(*values):
    return lax.optimization_barrier(values)


def shards(hidden_states, norm_gain, value_weight, queries, keys, readout, targets, scored):
    width = hidden_states.shape[1] * 2
    read = readout.reshape(HALF, HD)
    v = read_weight(value_weight, read)
    v = lax.all_to_all(v.reshape(64, 8, 128), FAR, 0, 0).reshape(512, 128)
    v, norm_gain, targets, scored, value_weight = together(v, norm_gain, targets, scored, value_weight)
    gain = norm_gain[None]
    own, send = whole(pick_kernel, [shape(256, 128, dtype=BF16)] * 2, v)
    own_y = swap(send, "yl")
    got = swap(own, "core")
    x, probs, ss = early(hidden_states, queries, keys, v)
    own_y, got, ss = together(own_y, got, ss)
    got_y = swap(own_y, "core")
    gvt, u, send = project((own, own_y, got, got_y), gain, x, ss)
    send, weight = together(send, value_weight)
    got, weight = together(swap(send, "yl"), cross(weight))
    part, u, rms = make_values(width, probs, u, got, ss)
    part, weight = together(part, weight)
    got, other_weight = together(swap(part, "yl"), swap(weight, "yh"))
    values, c = make_error(probs, u, part, got, targets[None], scored[None])
    c, dot, keep, send = make_rows(c, swap(c, "yl"), rms, x)
    z = (keep + swap(send, "core")).astype(BF16).reshape(32, HALF, 128)
    z = lax.all_to_all(z, PLANE, 0, 0)
    grad_input, log_scale = input_grad(width, c, dot, rms, gvt, x, z)
    tails = whole(sum_kernel, shape(8, HALF + 16, 128), z, gain, own, own_y, weight, other_weight)
    tails = lax.all_to_all(tails, NEAR, 0, 0)
    tails, z = whole(near_kernel, [shape(32, HALF + 8, 128, dtype=BF16), shape(8, 128)], tails)
    grad_weight = whole(weight_kernel, shape(ROWS, 2 * HD), z, read)
    tails = lax.all_to_all(tails, PLANE, 0, 0)
    grad_readout, grad_gain = whole(last_kernel, [shape(HALF, HD), shape(32, 128)], tails)
    return (values[0], grad_input, grad_weight, grad_gain.reshape(-1), grad_readout.reshape(-1), log_scale[0])


def solution(mesh):
    fine = Mesh(mesh.devices.reshape(2, 4, 2, 8, 2), ("yh", "x", "core", "z", "yl"))
    seq = ("yh", "x", "core", "z")
    return jax.shard_map(
        shards,
        mesh=fine,
        in_specs=(
            P(seq, "yl"),
            P("yl"),
            P(seq, "yl"),
            P(seq, "yl"),
            P(seq, "yl"),
            P("yl"),
            P(seq),
            P(seq),
        ),
        out_specs=(
            P(seq),
            P(seq, "yl"),
            P(seq, "yl"),
            P("yl"),
            P("yl"),
            P(seq),
        ),
        check_vma=False,
    )
```

```python
import jax
import jax.numpy as jnp
from jax import lax
from jax.experimental import pallas as pl
from jax.experimental.pallas import tpu as pltpu
from jax.sharding import Mesh
from jax.sharding import PartitionSpec as P

HD = 128
GROUP = 8
EPS = 1e-06
F32 = jnp.float32
BF16 = jnp.bfloat16
HIGHEST = lax.Precision.HIGHEST
VMEM = pl.BlockSpec(memory_space=pltpu.VMEM)
HBM = pl.BlockSpec(memory_space=pltpu.HBM)
ANY = pl.BlockSpec(memory_space=pl.ANY)
LOADS = pltpu.CompilerParams(vmem_limit_bytes=51 * 1024 * 1024)
PARAMS = pltpu.CompilerParams(vmem_limit_bytes=16 * 1024 * 1024)


PLANE = ("x", "z")
NEAR = ("yh", "core", "yl")
ROWS = 64
BLOCKS = 64
HALF = 16


def swap(v, axis):
    return lax.ppermute(v, axis, [(0, 1), (1, 0)])


def cross(v):
    return lax.ppermute(v, ("yh", "yl"), [(0, 0), (1, 2), (2, 1), (3, 3)])


def split(bit, v, axis):
    n = v.shape[axis] // 2
    low = lax.slice_in_dim(v, 0, n, axis=axis)
    high = lax.slice_in_dim(v, n, 2 * n, axis=axis)
    return jnp.where(bit, high, low), jnp.where(bit, low, high)


def whole(body, out_shape, *args, scratch=()):
    many = isinstance(out_shape, list)
    return pl.pallas_call(
        body,
        in_specs=[VMEM] * len(args),
        out_specs=[VMEM] * len(out_shape) if many else VMEM,
        out_shape=out_shape,
        scratch_shapes=scratch,
        compiler_params=PARAMS,
    )(*args)


def shape(*dims, dtype=F32):
    return jax.ShapeDtypeStruct(dims, dtype)


def exact_dot(a, b, dims):
    return lax.dot_general(a, b, (dims, ((), ())), precision=HIGHEST, preferred_element_type=F32)


def left_lanes(rows):
    return lax.broadcasted_iota(jnp.int32, (rows, 128), 1) < 64


def read_kernel(w_ref, r_ref, v_ref, w2_ref):
    parts = []
    for g in range(2):
        w = w_ref[:, g * HD : (g + 1) * HD]
        w2_ref[g * ROWS : (g + 1) * ROWS] = w
        parts.append(exact_dot(r_ref[g * GROUP : (g + 1) * GROUP], w.astype(F32), ((1,), (1,))))
    v = jnp.concatenate(parts, axis=1)
    v = jnp.concatenate([v, v], axis=0).astype(BF16)
    for i in range(16):
        v_ref[i * 16 : (i + 1) * 16] = v


def stack_kernel(v_ref, w_ref, out_ref):
    out_ref[:256] = v_ref[...]
    out_ref[256:] = w_ref[...]


def merge_kernel(self_ref, ring_ref, swap_ref, v_ref, w_ref):
    straight = lax.axis_index("yh") == lax.axis_index("yl")
    ring = ring_ref[...]
    own = jnp.where(straight, self_ref[...], ring)
    other = jnp.where(straight, ring, swap_ref[...])
    v_ref[:256] = own[:256]
    v_ref[256:] = other[:256]
    w_ref[:128] = own[256:]
    w_ref[128:] = other[256:]


def row_sum_of_transpose(a):
    return jnp.sum(a.T, axis=0, keepdims=True)


def load_kernel(x_ref, after_ref, xv_ref, ss_ref, sem):
    copy = pltpu.make_async_copy(x_ref, xv_ref, sem)
    copy.start()
    copy.wait()
    total = jnp.zeros((xv_ref.shape[0], 128), F32)
    for b in range(xv_ref.shape[1] // 128):
        xb = xv_ref[:, b * 128 : (b + 1) * 128].astype(F32)
        total += xb * xb
    ss_ref[...] = row_sum_of_transpose(total)


def load(x, after):
    return pl.pallas_call(
        load_kernel,
        in_specs=[HBM, ANY],
        out_specs=[VMEM] * 2,
        out_shape=[shape(*x.shape, dtype=BF16), shape(1, x.shape[0])],
        scratch_shapes=[pltpu.SemaphoreType.DMA],
        compiler_params=LOADS,
    )(x, after)


def attention_kernel(q_ref, k_ref, after_ref, p_ref):
    length = q_ref.shape[0]
    rows = lax.broadcasted_iota(jnp.int32, (length, length), 0)
    cols = lax.broadcasted_iota(jnp.int32, (length, length), 1)
    allowed = cols <= rows
    for h in range(HALF):
        g = h // GROUP
        s = lax.dot_general(
            q_ref[:, h * HD : (h + 1) * HD],
            k_ref[:, g * HD : (g + 1) * HD],
            (((1,), (1,)), ((), ())),
            preferred_element_type=F32,
        )
        s = jnp.where(allowed, s * (HD**-0.5), -1e30)
        e = jnp.exp(s - jnp.max(s, axis=1, keepdims=True))
        p_ref[h] = (e / jnp.sum(e, axis=1, keepdims=True)).astype(BF16)


def attention(queries, keys, after):
    length = queries.shape[0]
    return whole(attention_kernel, shape(HALF, length, length, dtype=BF16), queries, keys, after)


def project_kernel(
    own_ref, got_ref, gain_ref, x_ref, ss_ref, gvt_ref, u_ref, send_ref
):
    core = lax.axis_index("core")
    low = left_lanes(8)
    for b in range(BLOCKS // 2):
        xi, c, zp = b // 8, b // 4 % 2, b % 4
        at = slice(b * 128, (b + 1) * 128)
        halves = []
        for h in range(2):
            row = h * 256 + (xi * 8 + 2 * zp) * 8
            pair = jnp.where(
                core == c, own_ref[row : row + 16].astype(F32), got_ref[row : row + 16].astype(F32)
            )
            one, two = pair[:8], pair[8:]
            halves.append(jnp.where(low, one, pltpu.roll(two, 64, 1)))
            halves.append(jnp.where(low, pltpu.roll(one, 64, 1), two))
        vt = jnp.concatenate(halves, axis=0)
        gvt_ref[:, at] = (vt * gain_ref[:, at].astype(F32)).astype(BF16)
    u = lax.dot_general(
        gvt_ref[...], x_ref[...], (((1,), (1,)), ((), ())), preferred_element_type=F32
    )
    u_ref[...] = u[:HALF]
    send_ref[:HALF] = u[HALF:]
    send_ref[HALF:] = jnp.broadcast_to(ss_ref[...], (8, u.shape[1]))


def project(own, got, gain, x, ss):
    length, wide = x.shape
    return whole(
        project_kernel,
        [shape(32, wide, dtype=BF16), shape(HALF, length), shape(HALF + 8, length)],
        own, got, gain, x, ss,
    )


def values_kernel(width, p_ref, own_ref, got_ref, ss_ref, v_ref, u_ref, rms_ref):
    got = got_ref[...]
    rms = lax.rsqrt((ss_ref[...] + got[HALF : HALF + 1]) / width + EPS)
    rms_ref[...] = rms
    u = own_ref[...] + got[:HALF]
    u_ref[...] = u
    u = u * rms
    total = jnp.zeros(p_ref.shape[1:], F32)
    for j in range(HALF):
        total += p_ref[j].astype(F32) * u[j : j + 1]
    v_ref[...] = row_sum_of_transpose(total)


def make_values(width, probs, own, got, ss):
    length = probs.shape[1]
    return whole(
        lambda *refs: values_kernel(width, *refs),
        [shape(1, length), shape(HALF, length), shape(1, length)],
        probs, own, got, ss,
    )


def error_kernel(p_ref, u_ref, own_ref, got_ref, targets_ref, scored_ref, values_ref, c_ref):
    length = u_ref.shape[1]
    values = own_ref[...] + got_ref[...]
    values_ref[...] = values
    error = (values - targets_ref[...]) * scored_ref[...].astype(F32)
    high = error.astype(BF16)
    low = (error - high.astype(F32)).astype(BF16)
    both = jnp.concatenate([jnp.broadcast_to(high, (8, length)), jnp.broadcast_to(low, (8, length))], axis=0)
    rows = []
    for j in range(HALF):
        c = jnp.dot(both, p_ref[j], preferred_element_type=F32)
        rows.append(c[:1] + c[8:9])
    c = jnp.concatenate(rows, axis=0)
    c_ref[:HALF] = c
    c_ref[HALF:] = jnp.broadcast_to(jnp.sum(c * u_ref[...], axis=0, keepdims=True), (8, length))


def make_error(probs, u, own, got, targets, scored):
    length = probs.shape[1]
    return whole(
        error_kernel, [shape(1, length), shape(HALF + 8, length)], probs, u, own, got, targets, scored
    )


def rows_kernel(own_ref, got_ref, rms_ref, x_ref, c_ref, dot_ref, keep_ref, send_ref):
    core = lax.axis_index("core")
    c = jnp.concatenate([own_ref[:HALF], got_ref[:HALF]], axis=0) * rms_ref[...]
    c_ref[...] = c
    dot_ref[...] = own_ref[HALF : HALF + 1] + got_ref[HALF : HALF + 1]
    high = c.astype(BF16)
    low = (c - high.astype(F32)).astype(BF16)
    both = jnp.concatenate([high, low], axis=0)
    z = jnp.dot(both, x_ref[...], preferred_element_type=F32)
    z = z[:32] + z[32:]
    left = left_lanes(8)

    def chunks(b):
        at = slice(b * 128, (b + 1) * 128)
        parts = [z[i * 8 : (i + 1) * 8, at] for i in range(4)]
        even = [jnp.where(left, parts[i], pltpu.roll(parts[i + 1], 64, 1)) for i in (0, 2)]
        odd = [jnp.where(left, pltpu.roll(parts[i], 64, 1), parts[i + 1]) for i in (0, 2)]
        return jnp.concatenate([*even, *odd], axis=0)

    for xi in range(4):
        for zp in range(4):
            at = pl.ds((xi * 4 + zp) * 32, 32)
            zero, one = chunks(xi * 8 + zp), chunks(xi * 8 + 4 + zp)
            keep_ref[at] = jnp.where(core == 0, zero, one)
            send_ref[at] = jnp.where(core == 0, one, zero).astype(BF16)


def make_rows(own, got, rms, x):
    length = x.shape[0]
    return whole(
        rows_kernel,
        [shape(32, length), shape(1, length), shape(512, 128), shape(512, 128, dtype=BF16)],
        own, got, rms, x,
    )


def sum_kernel(parts_ref, gain_ref, v_ref, w_ref, tails_ref):
    side = lax.axis_index("yl")
    xi, zi = lax.axis_index("x"), lax.axis_index("z")
    even = zi % 2 == 0
    vs = []
    for h in range(2):
        at = pl.ds(pl.multiple_of(h * 256 + (xi * 4 + zi // 2) * 16, 16), 16)
        pair = v_ref[at].astype(F32)
        vs.append(jnp.where(even, pair[:8], pair[8:]))
    v = jnp.concatenate(vs, axis=0)
    spot = (xi * 2 + lax.axis_index("core")) * 4 + zi // 2
    gain = jnp.zeros((1, 128), F32)
    for b in range(BLOCKS // 2):
        gain = jnp.where(spot == b, gain_ref[:, b * 128 : (b + 1) * 128].astype(F32), gain)
    gain = jnp.where(left_lanes(1) == even, gain, pltpu.roll(gain, 64, 1))
    total = jnp.zeros((HALF, 128), F32)
    for b in range(32):
        total += parts_ref[b].astype(F32)
    z = total * gain
    part = jnp.sum(total * v, axis=0, keepdims=True)
    part = jnp.broadcast_to(part + pltpu.roll(part, 64, 1), (8, 128))
    ws = [w_ref[i * ROWS : (i + 1) * ROWS].astype(F32) for i in range(4)]
    tails = []
    for h in range(2):
        rows = z[h * 8 : (h + 1) * 8]
        reads = []
        for g in range(2):
            reads.append(exact_dot(rows[:, g * ROWS : (g + 1) * ROWS], ws[2 * h + g], ((1,), (0,))))
        tails.append(jnp.concatenate([*reads, part, rows], axis=0))
    for i in range(8):
        tails_ref[i] = jnp.where(side == i % 2, tails[0], tails[1])


def weight_kernel(z_ref, r_ref, grad_ref):
    for g in range(2):
        z = z_ref[:, g * ROWS : (g + 1) * ROWS]
        grad_ref[:, g * HD : (g + 1) * HD] = exact_dot(z, r_ref[g * GROUP : (g + 1) * GROUP], ((0,), (0,)))


def near_kernel(tails_ref, out_ref, z_ref):
    core, side, far = lax.axis_index("core"), lax.axis_index("yl"), lax.axis_index("yh")
    read = tails_ref[0][:HALF]
    for i in range(1, 8):
        read += tails_ref[i][:HALF]
    gain = slice(HALF, HALF + 8)
    zero = tails_ref[side][gain] + tails_ref[4 + side][gain]
    one = tails_ref[2 + side][gain] + tails_ref[6 + side][gain]
    at = 2 * core + far
    z_ref[...] = tails_ref[at][HALF + 8 :] + tails_ref[4 + at][HALF + 8 :]
    tail = jnp.concatenate([read, jnp.where(left_lanes(8), zero, one)], axis=0).astype(BF16)
    for i in range(32):
        out_ref[i] = tail


def last_kernel(all_ref, read_ref, gain_ref):
    left = left_lanes(1)
    total = all_ref[0].astype(F32)
    for i in range(1, 32):
        total += all_ref[i].astype(F32)
    read_ref[...] = total[:HALF]
    for xi in range(4):
        for zp in range(4):
            i = xi * 8 + 2 * zp
            one = all_ref[i].astype(F32)[HALF : HALF + 1]
            two = all_ref[i + 1].astype(F32)[HALF : HALF + 1]
            row = xi * 8 + zp
            gain_ref[row : row + 1] = jnp.where(left, one, pltpu.roll(two, 64, 1))
            gain_ref[row + 4 : row + 5] = jnp.where(left, pltpu.roll(one, 64, 1), two)


def input_kernel(width, c_ref, dot_ref, rms_ref, gvt_ref, x_ref, after_ref, out_ref, log_ref):
    rms = rms_ref[...]
    length = rms.shape[1]
    c = c_ref[...]
    high = c.astype(BF16)
    low = (c - high.astype(F32)).astype(BF16)
    log_scale = rms * dot_ref[...]
    log_ref[...] = log_scale
    back = jnp.broadcast_to(rms * rms * log_scale / width, (128, length)).T
    gvt = gvt_ref[...]
    grad = lax.dot_general(
        jnp.concatenate([high, low], axis=0),
        jnp.concatenate([gvt, gvt], axis=0),
        (((0,), (0,)), ((), ())),
        preferred_element_type=F32,
    )
    for b in range(grad.shape[1] // 128):
        at = slice(b * 128, (b + 1) * 128)
        out_ref[:, at] = (grad[:, at] - x_ref[:, at].astype(F32) * back).astype(BF16)


def input_grad(width, c, dot, rms, gvt, x, after):
    steps = 4
    length, wide = x.shape
    return pl.pallas_call(
        lambda *refs: input_kernel(width, *refs),
        grid=(steps,),
        in_specs=[
            pl.BlockSpec((32, length), lambda i: (0, 0)),
            pl.BlockSpec((1, length), lambda i: (0, 0)),
            pl.BlockSpec((1, length), lambda i: (0, 0)),
            pl.BlockSpec((32, wide // steps), lambda i: (0, i)),
            pl.BlockSpec((length, wide // steps), lambda i: (0, i)),
            ANY,
        ],
        out_specs=[
            pl.BlockSpec((length, wide // steps), lambda i: (0, i)),
            pl.BlockSpec((1, length), lambda i: (0, 0)),
        ],
        out_shape=[shape(length, wide, dtype=BF16), shape(1, length)],
        compiler_params=PARAMS,
    )(c, dot, rms, gvt, x, after)


def together(*values):
    return lax.optimization_barrier(values)


def shards(hidden_states, norm_gain, value_weight, queries, keys, readout, targets, scored):
    width = hidden_states.shape[1] * 2
    read = readout.reshape(HALF, HD)
    v, w = whole(
        read_kernel, [shape(256, 128, dtype=BF16), shape(128, 128, dtype=BF16)], value_weight, read
    )
    v = lax.all_to_all(v.reshape(32, 8, 128), PLANE, 0, 0).reshape(256, 128)
    v, norm_gain, targets, scored = together(v, norm_gain, targets, scored)
    gain = norm_gain[None]
    both = whole(stack_kernel, shape(384, 128, dtype=BF16), v, w)
    first = lax.ppermute(both, ("yh", "yl"), [(1, 0), (0, 2), (2, 3), (3, 1)])
    second = lax.ppermute(both, ("yh", "yl"), [(1, 2), (2, 1)])
    x, ss = load(hidden_states, v)
    first, second, ss = together(first, second, ss)
    v, weight = whole(
        merge_kernel, [shape(512, 128, dtype=BF16), shape(256, 128, dtype=BF16)], both, first, second
    )
    gvt, u, send = project(v, swap(v, "core"), gain, x, ss)
    probs = attention(queries, keys, u)
    part, u, rms = make_values(width, probs, u, swap(send, "yl"), ss)
    got = swap(part, "yl")
    values, c = make_error(probs, u, part, got, targets[None], scored[None])
    c, dot, keep, send = make_rows(c, swap(c, "yl"), rms, x)
    z = (keep + swap(send, "core").astype(F32)).astype(BF16).reshape(32, HALF, 128)
    z = lax.all_to_all(z, PLANE, 0, 0)
    grad_input, log_scale = input_grad(width, c, dot, rms, gvt, x, z)
    tails = whole(sum_kernel, shape(8, HALF + 16, 128), z, gain, v, weight)
    tails = lax.all_to_all(tails, NEAR, 0, 0)
    tails, z = whole(near_kernel, [shape(32, HALF + 8, 128, dtype=BF16), shape(8, 128)], tails)
    grad_weight = whole(weight_kernel, shape(ROWS, 2 * HD), z, read)
    tails = lax.all_to_all(tails, PLANE, 0, 0)
    grad_readout, grad_gain = whole(last_kernel, [shape(HALF, HD), shape(32, 128)], tails)
    return (values[0], grad_input, grad_weight, grad_gain.reshape(-1), grad_readout.reshape(-1), log_scale[0])


def solution(mesh):
    fine = Mesh(mesh.devices.reshape(2, 4, 2, 8, 2), ("yh", "x", "core", "z", "yl"))
    seq = ("yh", "x", "core", "z")
    return jax.shard_map(
        shards,
        mesh=fine,
        in_specs=(
            P(seq, "yl"),
            P("yl"),
            P(seq, "yl"),
            P(seq, "yl"),
            P(seq, "yl"),
            P("yl"),
            P(seq),
            P(seq),
        ),
        out_specs=(
            P(seq),
            P(seq, "yl"),
            P(seq, "yl"),
            P("yl"),
            P("yl"),
            P(seq),
        ),
        check_vma=False,
    )
```

```python
import jax
import jax.numpy as jnp
from jax import lax
from jax.experimental import pallas as pl
from jax.experimental.pallas import tpu as pltpu
from jax.sharding import Mesh
from jax.sharding import PartitionSpec as P

HD = 128
GROUP = 8
EPS = 1e-06
F32 = jnp.float32
BF16 = jnp.bfloat16
HIGHEST = lax.Precision.HIGHEST
VMEM = pl.BlockSpec(memory_space=pltpu.VMEM)
HBM = pl.BlockSpec(memory_space=pltpu.HBM)
ANY = pl.BlockSpec(memory_space=pl.ANY)
LOADS = pltpu.CompilerParams(vmem_limit_bytes=51 * 1024 * 1024)
PARAMS = pltpu.CompilerParams(vmem_limit_bytes=16 * 1024 * 1024)


PLANE = ("x", "z")
NEAR = ("yh", "core", "yl")
ROWS = 64
BLOCKS = 64
HALF = 16


def swap(v, axis):
    return lax.ppermute(v, axis, [(0, 1), (1, 0)])


def cross(v):
    return lax.ppermute(v, ("yh", "yl"), [(0, 0), (1, 2), (2, 1), (3, 3)])


def split(bit, v, axis):
    n = v.shape[axis] // 2
    low = lax.slice_in_dim(v, 0, n, axis=axis)
    high = lax.slice_in_dim(v, n, 2 * n, axis=axis)
    return jnp.where(bit, high, low), jnp.where(bit, low, high)


def whole(body, out_shape, *args, scratch=()):
    many = isinstance(out_shape, list)
    return pl.pallas_call(
        body,
        in_specs=[VMEM] * len(args),
        out_specs=[VMEM] * len(out_shape) if many else VMEM,
        out_shape=out_shape,
        scratch_shapes=scratch,
        compiler_params=PARAMS,
    )(*args)


def shape(*dims, dtype=F32):
    return jax.ShapeDtypeStruct(dims, dtype)


def exact_dot(a, b, dims):
    return lax.dot_general(a, b, (dims, ((), ())), precision=HIGHEST, preferred_element_type=F32)


def left_lanes(rows):
    return lax.broadcasted_iota(jnp.int32, (rows, 128), 1) < 64


def read_kernel(w_ref, r_ref, out_ref):
    parts = []
    for g in range(2):
        w = w_ref[:, g * HD : (g + 1) * HD]
        out_ref[g * ROWS : (g + 1) * ROWS] = w
        parts.append(exact_dot(r_ref[g * GROUP : (g + 1) * GROUP], w.astype(F32), ((1,), (1,))))
    v = jnp.concatenate(parts, axis=1)
    out_ref[128:] = jnp.concatenate([v, v], axis=0).astype(BF16)


def merge_kernel(self_ref, ring_ref, swap_ref, v_ref, w_ref):
    straight = lax.axis_index("yh") == lax.axis_index("yl")
    ring = ring_ref[...]
    own = jnp.where(straight, self_ref[...], ring)
    other = jnp.where(straight, ring, swap_ref[...])
    w_ref[:128] = own[:128]
    w_ref[128:] = other[:128]
    upper = lax.broadcasted_iota(jnp.int32, (16, 128), 0) < 8
    v = jnp.where(upper, own[128:].astype(F32), other[128:].astype(F32)).astype(BF16)
    for i in range(32):
        v_ref[i * 16 : (i + 1) * 16] = v


def row_sum_of_transpose(a):
    return jnp.sum(a.T, axis=0, keepdims=True)


def load_kernel(x_ref, after_ref, xv_ref, ss_ref, sem):
    copy = pltpu.make_async_copy(x_ref, xv_ref, sem)
    copy.start()
    copy.wait()
    total = jnp.zeros((xv_ref.shape[0], 128), F32)
    for b in range(xv_ref.shape[1] // 128):
        xb = xv_ref[:, b * 128 : (b + 1) * 128].astype(F32)
        total += xb * xb
    ss_ref[...] = row_sum_of_transpose(total)


def load(x, after):
    return pl.pallas_call(
        load_kernel,
        in_specs=[HBM, ANY],
        out_specs=[VMEM] * 2,
        out_shape=[shape(*x.shape, dtype=BF16), shape(1, x.shape[0])],
        scratch_shapes=[pltpu.SemaphoreType.DMA],
        compiler_params=LOADS,
    )(x, after)


def attention_kernel(q_ref, k_ref, after_ref, p_ref):
    length = q_ref.shape[0]
    rows = lax.broadcasted_iota(jnp.int32, (length, length), 0)
    cols = lax.broadcasted_iota(jnp.int32, (length, length), 1)
    allowed = cols <= rows
    for h in range(HALF):
        g = h // GROUP
        s = lax.dot_general(
            q_ref[:, h * HD : (h + 1) * HD],
            k_ref[:, g * HD : (g + 1) * HD],
            (((1,), (1,)), ((), ())),
            preferred_element_type=F32,
        )
        s = jnp.where(allowed, s * (HD**-0.5), -1e30)
        e = jnp.exp(s - jnp.max(s, axis=1, keepdims=True))
        p_ref[h] = (e / jnp.sum(e, axis=1, keepdims=True)).astype(BF16)


def attention(queries, keys, after):
    length = queries.shape[0]
    return whole(attention_kernel, shape(HALF, length, length, dtype=BF16), queries, keys, after)


def project_kernel(
    own_ref, got_ref, gain_ref, x_ref, ss_ref, gvt_ref, u_ref, send_ref
):
    core = lax.axis_index("core")
    low = left_lanes(8)
    for b in range(BLOCKS // 2):
        xi, c, zp = b // 8, b // 4 % 2, b % 4
        at = slice(b * 128, (b + 1) * 128)
        row = (xi * 8 + 2 * zp) * 16
        quad = jnp.where(
            core == c, own_ref[row : row + 32].astype(F32), got_ref[row : row + 32].astype(F32)
        )
        halves = []
        for h in range(2):
            one, two = quad[h * 8 : h * 8 + 8], quad[h * 8 + 16 : h * 8 + 24]
            halves.append(jnp.where(low, one, pltpu.roll(two, 64, 1)))
            halves.append(jnp.where(low, pltpu.roll(one, 64, 1), two))
        vt = jnp.concatenate(halves, axis=0)
        gvt_ref[:, at] = (vt * gain_ref[:, at].astype(F32)).astype(BF16)
    u = lax.dot_general(
        gvt_ref[...], x_ref[...], (((1,), (1,)), ((), ())), preferred_element_type=F32
    )
    u_ref[...] = u[:HALF]
    send_ref[:HALF] = u[HALF:]
    send_ref[HALF:] = jnp.broadcast_to(ss_ref[...], (8, u.shape[1]))


def project(own, got, gain, x, ss):
    length, wide = x.shape
    return whole(
        project_kernel,
        [shape(32, wide, dtype=BF16), shape(HALF, length), shape(HALF + 8, length)],
        own, got, gain, x, ss,
    )


def values_kernel(width, p_ref, own_ref, got_ref, ss_ref, v_ref, u_ref, rms_ref):
    got = got_ref[...]
    rms = lax.rsqrt((ss_ref[...] + got[HALF : HALF + 1]) / width + EPS)
    rms_ref[...] = rms
    u = own_ref[...] + got[:HALF]
    u_ref[...] = u
    u = u * rms
    total = jnp.zeros(p_ref.shape[1:], F32)
    for j in range(HALF):
        total += p_ref[j].astype(F32) * u[j : j + 1]
    v_ref[...] = row_sum_of_transpose(total)


def make_values(width, probs, own, got, ss):
    length = probs.shape[1]
    return whole(
        lambda *refs: values_kernel(width, *refs),
        [shape(1, length), shape(HALF, length), shape(1, length)],
        probs, own, got, ss,
    )


def error_kernel(p_ref, u_ref, own_ref, got_ref, targets_ref, scored_ref, values_ref, c_ref):
    length = u_ref.shape[1]
    values = own_ref[...] + got_ref[...]
    values_ref[...] = values
    error = (values - targets_ref[...]) * scored_ref[...].astype(F32)
    high = error.astype(BF16)
    low = (error - high.astype(F32)).astype(BF16)
    both = jnp.concatenate([jnp.broadcast_to(high, (8, length)), jnp.broadcast_to(low, (8, length))], axis=0)
    rows = []
    for j in range(HALF):
        c = jnp.dot(both, p_ref[j], preferred_element_type=F32)
        rows.append(c[:1] + c[8:9])
    c = jnp.concatenate(rows, axis=0)
    c_ref[:HALF] = c
    c_ref[HALF:] = jnp.broadcast_to(jnp.sum(c * u_ref[...], axis=0, keepdims=True), (8, length))


def make_error(probs, u, own, got, targets, scored):
    length = probs.shape[1]
    return whole(
        error_kernel, [shape(1, length), shape(HALF + 8, length)], probs, u, own, got, targets, scored
    )


def rows_kernel(own_ref, got_ref, rms_ref, x_ref, c_ref, dot_ref, keep_ref, send_ref):
    core = lax.axis_index("core")
    c = jnp.concatenate([own_ref[:HALF], got_ref[:HALF]], axis=0) * rms_ref[...]
    c_ref[...] = c
    dot_ref[...] = own_ref[HALF : HALF + 1] + got_ref[HALF : HALF + 1]
    high = c.astype(BF16)
    low = (c - high.astype(F32)).astype(BF16)
    both = jnp.concatenate([high, low], axis=0)
    z = jnp.dot(both, x_ref[...], preferred_element_type=F32)
    z = z[:32] + z[32:]
    left = left_lanes(8)

    def chunks(b):
        at = slice(b * 128, (b + 1) * 128)
        parts = [z[i * 8 : (i + 1) * 8, at] for i in range(4)]
        even = [jnp.where(left, parts[i], pltpu.roll(parts[i + 1], 64, 1)) for i in (0, 2)]
        odd = [jnp.where(left, pltpu.roll(parts[i], 64, 1), parts[i + 1]) for i in (0, 2)]
        return jnp.concatenate([*even, *odd], axis=0)

    for xi in range(4):
        for zp in range(4):
            at = pl.ds((xi * 4 + zp) * 32, 32)
            zero, one = chunks(xi * 8 + zp), chunks(xi * 8 + 4 + zp)
            keep_ref[at] = jnp.where(core == 0, zero, one)
            send_ref[at] = jnp.where(core == 0, one, zero).astype(BF16)


def make_rows(own, got, rms, x):
    length = x.shape[0]
    return whole(
        rows_kernel,
        [shape(32, length), shape(1, length), shape(512, 128), shape(512, 128, dtype=BF16)],
        own, got, rms, x,
    )


def sum_kernel(parts_ref, gain_ref, v_ref, w_ref, tails_ref):
    side = lax.axis_index("yl")
    xi, zi = lax.axis_index("x"), lax.axis_index("z")
    even = zi % 2 == 0
    v = v_ref[pl.ds(pl.multiple_of((xi * 8 + zi) * 16, 16), 16)].astype(F32)
    spot = (xi * 2 + lax.axis_index("core")) * 4 + zi // 2
    gain = jnp.zeros((1, 128), F32)
    for b in range(BLOCKS // 2):
        gain = jnp.where(spot == b, gain_ref[:, b * 128 : (b + 1) * 128].astype(F32), gain)
    gain = jnp.where(left_lanes(1) == even, gain, pltpu.roll(gain, 64, 1))
    total = jnp.zeros((HALF, 128), F32)
    for b in range(32):
        total += parts_ref[b].astype(F32)
    z = total * gain
    part = jnp.sum(total * v, axis=0, keepdims=True)
    part = jnp.broadcast_to(part + pltpu.roll(part, 64, 1), (8, 128))
    ws = [w_ref[i * ROWS : (i + 1) * ROWS].astype(F32) for i in range(4)]
    tails = []
    for h in range(2):
        rows = z[h * 8 : (h + 1) * 8]
        reads = []
        for g in range(2):
            reads.append(exact_dot(rows[:, g * ROWS : (g + 1) * ROWS], ws[2 * h + g], ((1,), (0,))))
        tails.append(jnp.concatenate([*reads, part, rows], axis=0))
    for i in range(8):
        tails_ref[i] = jnp.where(side == i % 2, tails[0], tails[1]).astype(BF16)


def weight_kernel(z_ref, r_ref, grad_ref):
    for g in range(2):
        z = z_ref[:, g * ROWS : (g + 1) * ROWS]
        grad_ref[:, g * HD : (g + 1) * HD] = exact_dot(z, r_ref[g * GROUP : (g + 1) * GROUP], ((0,), (0,)))


def near_kernel(tails_ref, out_ref, z_ref):
    core, side, far = lax.axis_index("core"), lax.axis_index("yl"), lax.axis_index("yh")
    read = tails_ref[0].astype(F32)[:HALF]
    for i in range(1, 8):
        read += tails_ref[i].astype(F32)[:HALF]

    def pair(i):
        return tails_ref[i].astype(F32) + tails_ref[4 + i].astype(F32)

    zero, one = pair(side)[HALF : HALF + 8], pair(2 + side)[HALF : HALF + 8]
    z_ref[...] = pair(2 * core + far)[HALF + 8 :]
    tail = jnp.concatenate([read, jnp.where(left_lanes(8), zero, one)], axis=0).astype(BF16)
    for i in range(32):
        out_ref[i] = tail


def last_kernel(all_ref, read_ref, gain_ref):
    left = left_lanes(1)
    total = all_ref[0].astype(F32)
    for i in range(1, 32):
        total += all_ref[i].astype(F32)
    read_ref[...] = total[:HALF]
    for xi in range(4):
        for zp in range(4):
            i = xi * 8 + 2 * zp
            one = all_ref[i].astype(F32)[HALF : HALF + 1]
            two = all_ref[i + 1].astype(F32)[HALF : HALF + 1]
            row = xi * 8 + zp
            gain_ref[row : row + 1] = jnp.where(left, one, pltpu.roll(two, 64, 1))
            gain_ref[row + 4 : row + 5] = jnp.where(left, pltpu.roll(one, 64, 1), two)


def input_kernel(width, c_ref, dot_ref, rms_ref, gvt_ref, x_ref, after_ref, out_ref, log_ref):
    rms = rms_ref[...]
    length = rms.shape[1]
    c = c_ref[...]
    high = c.astype(BF16)
    low = (c - high.astype(F32)).astype(BF16)
    log_scale = rms * dot_ref[...]
    log_ref[...] = log_scale
    back = jnp.broadcast_to(rms * rms * log_scale / width, (128, length)).T
    gvt = gvt_ref[...]
    grad = lax.dot_general(
        jnp.concatenate([high, low], axis=0),
        jnp.concatenate([gvt, gvt], axis=0),
        (((0,), (0,)), ((), ())),
        preferred_element_type=F32,
    )
    for b in range(grad.shape[1] // 128):
        at = slice(b * 128, (b + 1) * 128)
        out_ref[:, at] = (grad[:, at] - x_ref[:, at].astype(F32) * back).astype(BF16)


def input_grad(width, c, dot, rms, gvt, x, after):
    steps = 4
    length, wide = x.shape
    return pl.pallas_call(
        lambda *refs: input_kernel(width, *refs),
        grid=(steps,),
        in_specs=[
            pl.BlockSpec((32, length), lambda i: (0, 0)),
            pl.BlockSpec((1, length), lambda i: (0, 0)),
            pl.BlockSpec((1, length), lambda i: (0, 0)),
            pl.BlockSpec((32, wide // steps), lambda i: (0, i)),
            pl.BlockSpec((length, wide // steps), lambda i: (0, i)),
            ANY,
        ],
        out_specs=[
            pl.BlockSpec((length, wide // steps), lambda i: (0, i)),
            pl.BlockSpec((1, length), lambda i: (0, 0)),
        ],
        out_shape=[shape(length, wide, dtype=BF16), shape(1, length)],
        compiler_params=PARAMS,
    )(c, dot, rms, gvt, x, after)


def together(*values):
    return lax.optimization_barrier(values)


def shards(hidden_states, norm_gain, value_weight, queries, keys, readout, targets, scored):
    width = hidden_states.shape[1] * 2
    read = readout.reshape(HALF, HD)
    both = whole(read_kernel, shape(144, 128, dtype=BF16), value_weight, read)
    first = lax.ppermute(both, ("yh", "yl"), [(1, 0), (0, 2), (2, 3), (3, 1)])
    second = lax.ppermute(both, ("yh", "yl"), [(1, 2), (2, 1)])
    x, ss = load(hidden_states, both)
    first, second, ss = together(first, second, ss)
    v, weight = whole(
        merge_kernel, [shape(512, 128, dtype=BF16), shape(256, 128, dtype=BF16)], both, first, second
    )
    v = lax.all_to_all(v.reshape(32, HALF, 128), PLANE, 0, 0).reshape(512, 128)
    v, norm_gain, targets, scored = together(v, norm_gain, targets, scored)
    gain = norm_gain[None]
    gvt, u, send = project(v, swap(v, "core"), gain, x, ss)
    probs = attention(queries, keys, u)
    part, u, rms = make_values(width, probs, u, swap(send, "yl"), ss)
    got = swap(part, "yl")
    values, c = make_error(probs, u, part, got, targets[None], scored[None])
    c, dot, keep, send = make_rows(c, swap(c, "yl"), rms, x)
    z = (keep + swap(send, "core").astype(F32)).astype(BF16).reshape(32, HALF, 128)
    z = lax.all_to_all(z, PLANE, 0, 0)
    grad_input, log_scale = input_grad(width, c, dot, rms, gvt, x, z)
    tails = whole(sum_kernel, shape(8, HALF + 16, 128, dtype=BF16), z, gain, v, weight)
    tails = lax.all_to_all(tails, NEAR, 0, 0)
    tails, z = whole(near_kernel, [shape(32, HALF + 8, 128, dtype=BF16), shape(8, 128)], tails)
    grad_weight = whole(weight_kernel, shape(ROWS, 2 * HD), z, read)
    tails = lax.all_to_all(tails, PLANE, 0, 0)
    grad_readout, grad_gain = whole(last_kernel, [shape(HALF, HD), shape(32, 128)], tails)
    return (values[0], grad_input, grad_weight, grad_gain.reshape(-1), grad_readout.reshape(-1), log_scale[0])


def solution(mesh):
    fine = Mesh(mesh.devices.reshape(2, 4, 2, 8, 2), ("yh", "x", "core", "z", "yl"))
    seq = ("yh", "x", "core", "z")
    return jax.shard_map(
        shards,
        mesh=fine,
        in_specs=(
            P(seq, "yl"),
            P("yl"),
            P(seq, "yl"),
            P(seq, "yl"),
            P(seq, "yl"),
            P("yl"),
            P(seq),
            P(seq),
        ),
        out_specs=(
            P(seq),
            P(seq, "yl"),
            P(seq, "yl"),
            P("yl"),
            P("yl"),
            P(seq),
        ),
        check_vma=False,
    )
```

```python
import jax
import jax.numpy as jnp
from jax import lax
from jax.experimental import pallas as pl
from jax.experimental.pallas import tpu as pltpu
from jax.sharding import Mesh
from jax.sharding import PartitionSpec as P

HD = 128
GROUP = 8
EPS = 1e-06
F32 = jnp.float32
BF16 = jnp.bfloat16
HIGHEST = lax.Precision.HIGHEST
VMEM = pl.BlockSpec(memory_space=pltpu.VMEM)
HBM = pl.BlockSpec(memory_space=pltpu.HBM)
ANY = pl.BlockSpec(memory_space=pl.ANY)
LOADS = pltpu.CompilerParams(vmem_limit_bytes=51 * 1024 * 1024)
PARAMS = pltpu.CompilerParams(vmem_limit_bytes=16 * 1024 * 1024)


PLANE = ("x", "z")
NEAR = ("yh", "core", "yl")
ROWS = 64
BLOCKS = 64
HALF = 16


def swap(v, axis):
    return lax.ppermute(v, axis, [(0, 1), (1, 0)])


def cross(v):
    return lax.ppermute(v, ("yh", "yl"), [(0, 0), (1, 2), (2, 1), (3, 3)])


def split(bit, v, axis):
    n = v.shape[axis] // 2
    low = lax.slice_in_dim(v, 0, n, axis=axis)
    high = lax.slice_in_dim(v, n, 2 * n, axis=axis)
    return jnp.where(bit, high, low), jnp.where(bit, low, high)


def whole(body, out_shape, *args, scratch=()):
    many = isinstance(out_shape, list)
    return pl.pallas_call(
        body,
        in_specs=[VMEM] * len(args),
        out_specs=[VMEM] * len(out_shape) if many else VMEM,
        out_shape=out_shape,
        scratch_shapes=scratch,
        compiler_params=PARAMS,
    )(*args)


def shape(*dims, dtype=F32):
    return jax.ShapeDtypeStruct(dims, dtype)


def exact_dot(a, b, dims):
    return lax.dot_general(a, b, (dims, ((), ())), precision=HIGHEST, preferred_element_type=F32)


def left_lanes(rows):
    return lax.broadcasted_iota(jnp.int32, (rows, 128), 1) < 64


def read_kernel(ring_ref, swap_ref, r_ref, other_r_ref, v_ref, w_both_ref):
    straight = lax.axis_index("yh") == lax.axis_index("yl")
    ring, pair = ring_ref[...], swap_ref[...]
    own = jnp.where(straight, pair, ring)
    other = jnp.where(straight, ring, pair)
    parts = []
    for i, (w, r) in enumerate(((own, r_ref), (other, other_r_ref))):
        halves = []
        for g in range(2):
            wg = w[:, g * HD : (g + 1) * HD]
            w_both_ref[(2 * i + g) * ROWS : (2 * i + g + 1) * ROWS] = wg
            halves.append(exact_dot(r[g * GROUP : (g + 1) * GROUP], wg.astype(F32), ((1,), (1,))))
        parts.append(jnp.concatenate(halves, axis=1))
    v = jnp.concatenate(parts, axis=0).astype(BF16)
    for i in range(32):
        v_ref[i * 16 : (i + 1) * 16] = v


def row_sum_of_transpose(a):
    return jnp.sum(a.T, axis=0, keepdims=True)


def load_kernel(x_ref, after_ref, xv_ref, ss_ref, sem):
    copy = pltpu.make_async_copy(x_ref, xv_ref, sem)
    copy.start()
    copy.wait()
    total = jnp.zeros((xv_ref.shape[0], 128), F32)
    for b in range(xv_ref.shape[1] // 128):
        xb = xv_ref[:, b * 128 : (b + 1) * 128].astype(F32)
        total += xb * xb
    ss_ref[...] = row_sum_of_transpose(total)


def load(x, after):
    return pl.pallas_call(
        load_kernel,
        in_specs=[HBM, ANY],
        out_specs=[VMEM] * 2,
        out_shape=[shape(*x.shape, dtype=BF16), shape(1, x.shape[0])],
        scratch_shapes=[pltpu.SemaphoreType.DMA],
        compiler_params=LOADS,
    )(x, after)


def attention_kernel(q_ref, k_ref, after_ref, p_ref):
    length = q_ref.shape[0]
    rows = lax.broadcasted_iota(jnp.int32, (length, length), 0)
    cols = lax.broadcasted_iota(jnp.int32, (length, length), 1)
    allowed = cols <= rows
    for h in range(HALF):
        g = h // GROUP
        s = lax.dot_general(
            q_ref[:, h * HD : (h + 1) * HD],
            k_ref[:, g * HD : (g + 1) * HD],
            (((1,), (1,)), ((), ())),
            preferred_element_type=F32,
        )
        s = jnp.where(allowed, s * (HD**-0.5), -1e30)
        e = jnp.exp(s - jnp.max(s, axis=1, keepdims=True))
        p_ref[h] = (e / jnp.sum(e, axis=1, keepdims=True)).astype(BF16)


def attention(queries, keys, after):
    length = queries.shape[0]
    return whole(attention_kernel, shape(HALF, length, length, dtype=BF16), queries, keys, after)


def project_kernel(
    own_ref, got_ref, gain_ref, x_ref, ss_ref, gvt_ref, u_ref, send_ref
):
    core = lax.axis_index("core")
    low = left_lanes(8)
    for b in range(BLOCKS // 2):
        xi, c, zp = b // 8, b // 4 % 2, b % 4
        at = slice(b * 128, (b + 1) * 128)
        row = (xi * 8 + 2 * zp) * 16
        quad = jnp.where(
            core == c, own_ref[row : row + 32].astype(F32), got_ref[row : row + 32].astype(F32)
        )
        halves = []
        for h in range(2):
            one, two = quad[h * 8 : h * 8 + 8], quad[h * 8 + 16 : h * 8 + 24]
            halves.append(jnp.where(low, one, pltpu.roll(two, 64, 1)))
            halves.append(jnp.where(low, pltpu.roll(one, 64, 1), two))
        vt = jnp.concatenate(halves, axis=0)
        gvt_ref[:, at] = (vt * gain_ref[:, at].astype(F32)).astype(BF16)
    u = lax.dot_general(
        gvt_ref[...], x_ref[...], (((1,), (1,)), ((), ())), preferred_element_type=F32
    )
    u_ref[...] = u[:HALF]
    send_ref[:HALF] = u[HALF:]
    send_ref[HALF:] = jnp.broadcast_to(ss_ref[...], (8, u.shape[1]))


def project(own, got, gain, x, ss):
    length, wide = x.shape
    return whole(
        project_kernel,
        [shape(32, wide, dtype=BF16), shape(HALF, length), shape(HALF + 8, length)],
        own, got, gain, x, ss,
    )


def values_kernel(width, p_ref, own_ref, got_ref, ss_ref, v_ref, u_ref, rms_ref):
    got = got_ref[...]
    rms = lax.rsqrt((ss_ref[...] + got[HALF : HALF + 1]) / width + EPS)
    rms_ref[...] = rms
    u = own_ref[...] + got[:HALF]
    u_ref[...] = u
    u = u * rms
    total = jnp.zeros(p_ref.shape[1:], F32)
    for j in range(HALF):
        total += p_ref[j].astype(F32) * u[j : j + 1]
    v_ref[...] = row_sum_of_transpose(total)


def make_values(width, probs, own, got, ss):
    length = probs.shape[1]
    return whole(
        lambda *refs: values_kernel(width, *refs),
        [shape(1, length), shape(HALF, length), shape(1, length)],
        probs, own, got, ss,
    )


def error_kernel(p_ref, u_ref, own_ref, got_ref, targets_ref, scored_ref, values_ref, c_ref):
    length = u_ref.shape[1]
    values = own_ref[...] + got_ref[...]
    values_ref[...] = values
    error = (values - targets_ref[...]) * scored_ref[...].astype(F32)
    high = error.astype(BF16)
    low = (error - high.astype(F32)).astype(BF16)
    both = jnp.concatenate([jnp.broadcast_to(high, (8, length)), jnp.broadcast_to(low, (8, length))], axis=0)
    rows = []
    for j in range(HALF):
        c = jnp.dot(both, p_ref[j], preferred_element_type=F32)
        rows.append(c[:1] + c[8:9])
    c = jnp.concatenate(rows, axis=0)
    c_ref[:HALF] = c
    c_ref[HALF:] = jnp.broadcast_to(jnp.sum(c * u_ref[...], axis=0, keepdims=True), (8, length))


def make_error(probs, u, own, got, targets, scored):
    length = probs.shape[1]
    return whole(
        error_kernel, [shape(1, length), shape(HALF + 8, length)], probs, u, own, got, targets, scored
    )


def rows_kernel(own_ref, got_ref, rms_ref, x_ref, c_ref, dot_ref, keep_ref, send_ref):
    core = lax.axis_index("core")
    c = jnp.concatenate([own_ref[:HALF], got_ref[:HALF]], axis=0) * rms_ref[...]
    c_ref[...] = c
    dot_ref[...] = own_ref[HALF : HALF + 1] + got_ref[HALF : HALF + 1]
    high = c.astype(BF16)
    low = (c - high.astype(F32)).astype(BF16)
    both = jnp.concatenate([high, low], axis=0)
    z = jnp.dot(both, x_ref[...], preferred_element_type=F32)
    z = z[:32] + z[32:]
    left = left_lanes(8)

    def chunks(b):
        at = slice(b * 128, (b + 1) * 128)
        parts = [z[i * 8 : (i + 1) * 8, at] for i in range(4)]
        even = [jnp.where(left, parts[i], pltpu.roll(parts[i + 1], 64, 1)) for i in (0, 2)]
        odd = [jnp.where(left, pltpu.roll(parts[i], 64, 1), parts[i + 1]) for i in (0, 2)]
        return jnp.concatenate([*even, *odd], axis=0)

    for xi in range(4):
        for zp in range(4):
            at = pl.ds((xi * 4 + zp) * 32, 32)
            zero, one = chunks(xi * 8 + zp), chunks(xi * 8 + 4 + zp)
            keep_ref[at] = jnp.where(core == 0, zero, one)
            send_ref[at] = jnp.where(core == 0, one, zero).astype(BF16)


def make_rows(own, got, rms, x):
    length = x.shape[0]
    return whole(
        rows_kernel,
        [shape(32, length), shape(1, length), shape(512, 128), shape(512, 128, dtype=BF16)],
        own, got, rms, x,
    )


def sum_kernel(parts_ref, gain_ref, v_ref, w_ref, tails_ref):
    side = lax.axis_index("yl")
    xi, zi = lax.axis_index("x"), lax.axis_index("z")
    even = zi % 2 == 0
    v = v_ref[pl.ds(pl.multiple_of((xi * 8 + zi) * 16, 16), 16)].astype(F32)
    spot = (xi * 2 + lax.axis_index("core")) * 4 + zi // 2
    gain = jnp.zeros((1, 128), F32)
    for b in range(BLOCKS // 2):
        gain = jnp.where(spot == b, gain_ref[:, b * 128 : (b + 1) * 128].astype(F32), gain)
    gain = jnp.where(left_lanes(1) == even, gain, pltpu.roll(gain, 64, 1))
    total = jnp.zeros((HALF, 128), F32)
    for b in range(32):
        total += parts_ref[b].astype(F32)
    z = total * gain
    part = jnp.sum(total * v, axis=0, keepdims=True)
    part = jnp.broadcast_to(part + pltpu.roll(part, 64, 1), (8, 128))
    ws = [w_ref[i * ROWS : (i + 1) * ROWS].astype(F32) for i in range(4)]
    tails = []
    for h in range(2):
        rows = z[h * 8 : (h + 1) * 8]
        reads = []
        for g in range(2):
            reads.append(exact_dot(rows[:, g * ROWS : (g + 1) * ROWS], ws[2 * h + g], ((1,), (0,))))
        tails.append(jnp.concatenate([*reads, part, rows], axis=0))
    for i in range(8):
        tails_ref[i] = jnp.where(side == i % 2, tails[0], tails[1]).astype(BF16)


def weight_kernel(z_ref, r_ref, grad_ref):
    for g in range(2):
        z = z_ref[:, g * ROWS : (g + 1) * ROWS]
        grad_ref[:, g * HD : (g + 1) * HD] = exact_dot(z, r_ref[g * GROUP : (g + 1) * GROUP], ((0,), (0,)))


def near_kernel(tails_ref, out_ref, z_ref):
    core, side, far = lax.axis_index("core"), lax.axis_index("yl"), lax.axis_index("yh")
    read = tails_ref[0].astype(F32)[:HALF]
    for i in range(1, 8):
        read += tails_ref[i].astype(F32)[:HALF]

    def pair(i):
        return tails_ref[i].astype(F32) + tails_ref[4 + i].astype(F32)

    zero, one = pair(side)[HALF : HALF + 8], pair(2 + side)[HALF : HALF + 8]
    z_ref[...] = pair(2 * core + far)[HALF + 8 :]
    tail = jnp.concatenate([read, jnp.where(left_lanes(8), zero, one)], axis=0).astype(BF16)
    for i in range(32):
        out_ref[i] = tail


def last_kernel(all_ref, read_ref, gain_ref):
    left = left_lanes(1)
    total = all_ref[0].astype(F32)
    for i in range(1, 32):
        total += all_ref[i].astype(F32)
    read_ref[...] = total[:HALF]
    for xi in range(4):
        for zp in range(4):
            i = xi * 8 + 2 * zp
            one = all_ref[i].astype(F32)[HALF : HALF + 1]
            two = all_ref[i + 1].astype(F32)[HALF : HALF + 1]
            row = xi * 8 + zp
            gain_ref[row : row + 1] = jnp.where(left, one, pltpu.roll(two, 64, 1))
            gain_ref[row + 4 : row + 5] = jnp.where(left, pltpu.roll(one, 64, 1), two)


def input_kernel(width, c_ref, dot_ref, rms_ref, gvt_ref, x_ref, after_ref, out_ref, log_ref):
    rms = rms_ref[...]
    length = rms.shape[1]
    c = c_ref[...]
    high = c.astype(BF16)
    low = (c - high.astype(F32)).astype(BF16)
    log_scale = rms * dot_ref[...]
    log_ref[...] = log_scale
    back = jnp.broadcast_to(rms * rms * log_scale / width, (128, length)).T
    gvt = gvt_ref[...]
    grad = lax.dot_general(
        jnp.concatenate([high, low], axis=0),
        jnp.concatenate([gvt, gvt], axis=0),
        (((0,), (0,)), ((), ())),
        preferred_element_type=F32,
    )
    for b in range(grad.shape[1] // 128):
        at = slice(b * 128, (b + 1) * 128)
        out_ref[:, at] = (grad[:, at] - x_ref[:, at].astype(F32) * back).astype(BF16)


def input_grad(width, c, dot, rms, gvt, x, after):
    steps = 4
    length, wide = x.shape
    return pl.pallas_call(
        lambda *refs: input_kernel(width, *refs),
        grid=(steps,),
        in_specs=[
            pl.BlockSpec((32, length), lambda i: (0, 0)),
            pl.BlockSpec((1, length), lambda i: (0, 0)),
            pl.BlockSpec((1, length), lambda i: (0, 0)),
            pl.BlockSpec((32, wide // steps), lambda i: (0, i)),
            pl.BlockSpec((length, wide // steps), lambda i: (0, i)),
            ANY,
        ],
        out_specs=[
            pl.BlockSpec((length, wide // steps), lambda i: (0, i)),
            pl.BlockSpec((1, length), lambda i: (0, 0)),
        ],
        out_shape=[shape(length, wide, dtype=BF16), shape(1, length)],
        compiler_params=PARAMS,
    )(c, dot, rms, gvt, x, after)


def together(*values):
    return lax.optimization_barrier(values)


def shards(hidden_states, norm_gain, value_weight, queries, keys, readout, targets, scored):
    width = hidden_states.shape[1] * 2
    read = readout.reshape(HALF, HD)
    other_read = swap(read, "yl")
    ring = lax.ppermute(value_weight, ("yh", "yl"), [(1, 0), (0, 2), (2, 3), (3, 1)])
    pair = cross(value_weight)
    x, ss = load(hidden_states, norm_gain)
    ring, pair, other_read, ss = together(ring, pair, other_read, ss)
    v, weight = whole(
        read_kernel,
        [shape(512, 128, dtype=BF16), shape(256, 128, dtype=BF16)],
        ring, pair, read, other_read,
    )
    v = lax.all_to_all(v.reshape(32, HALF, 128), PLANE, 0, 0).reshape(512, 128)
    v, norm_gain, targets, scored = together(v, norm_gain, targets, scored)
    gain = norm_gain[None]
    gvt, u, send = project(v, swap(v, "core"), gain, x, ss)
    probs = attention(queries, keys, u)
    part, u, rms = make_values(width, probs, u, swap(send, "yl"), ss)
    got = swap(part, "yl")
    values, c = make_error(probs, u, part, got, targets[None], scored[None])
    c, dot, keep, send = make_rows(c, swap(c, "yl"), rms, x)
    z = (keep + swap(send, "core").astype(F32)).astype(BF16).reshape(32, HALF, 128)
    z = lax.all_to_all(z, PLANE, 0, 0)
    grad_input, log_scale = input_grad(width, c, dot, rms, gvt, x, z)
    tails = whole(sum_kernel, shape(8, HALF + 16, 128, dtype=BF16), z, gain, v, weight)
    tails = lax.all_to_all(tails, NEAR, 0, 0)
    tails, z = whole(near_kernel, [shape(32, HALF + 8, 128, dtype=BF16), shape(8, 128)], tails)
    grad_weight = whole(weight_kernel, shape(ROWS, 2 * HD), z, read)
    tails = lax.all_to_all(tails, PLANE, 0, 0)
    grad_readout, grad_gain = whole(last_kernel, [shape(HALF, HD), shape(32, 128)], tails)
    return (values[0], grad_input, grad_weight, grad_gain.reshape(-1), grad_readout.reshape(-1), log_scale[0])


def solution(mesh):
    fine = Mesh(mesh.devices.reshape(2, 4, 2, 8, 2), ("yh", "x", "core", "z", "yl"))
    seq = ("yh", "x", "core", "z")
    return jax.shard_map(
        shards,
        mesh=fine,
        in_specs=(
            P(seq, "yl"),
            P("yl"),
            P(seq, "yl"),
            P(seq, "yl"),
            P(seq, "yl"),
            P("yl"),
            P(seq),
            P(seq),
        ),
        out_specs=(
            P(seq),
            P(seq, "yl"),
            P(seq, "yl"),
            P("yl"),
            P("yl"),
            P(seq),
        ),
        check_vma=False,
    )
```

```python
import jax
import jax.numpy as jnp
from jax import lax
from jax.experimental import pallas as pl
from jax.experimental.pallas import tpu as pltpu
from jax.sharding import Mesh
from jax.sharding import PartitionSpec as P

HD = 128
GROUP = 8
EPS = 1e-06
F32 = jnp.float32
BF16 = jnp.bfloat16
HIGHEST = lax.Precision.HIGHEST
VMEM = pl.BlockSpec(memory_space=pltpu.VMEM)
HBM = pl.BlockSpec(memory_space=pltpu.HBM)
ANY = pl.BlockSpec(memory_space=pl.ANY)
LOADS = pltpu.CompilerParams(vmem_limit_bytes=51 * 1024 * 1024)
PARAMS = pltpu.CompilerParams(vmem_limit_bytes=16 * 1024 * 1024)


PLANE = ("x", "z")
NEAR = ("yh", "core", "yl")
ROWS = 64
BLOCKS = 64
HALF = 16


def swap(v, axis):
    return lax.ppermute(v, axis, [(0, 1), (1, 0)])


def cross(v):
    return lax.ppermute(v, ("yh", "yl"), [(0, 0), (1, 2), (2, 1), (3, 3)])


def split(bit, v, axis):
    n = v.shape[axis] // 2
    low = lax.slice_in_dim(v, 0, n, axis=axis)
    high = lax.slice_in_dim(v, n, 2 * n, axis=axis)
    return jnp.where(bit, high, low), jnp.where(bit, low, high)


def whole(body, out_shape, *args, scratch=()):
    many = isinstance(out_shape, list)
    return pl.pallas_call(
        body,
        in_specs=[VMEM] * len(args),
        out_specs=[VMEM] * len(out_shape) if many else VMEM,
        out_shape=out_shape,
        scratch_shapes=scratch,
        compiler_params=PARAMS,
    )(*args)


def shape(*dims, dtype=F32):
    return jax.ShapeDtypeStruct(dims, dtype)


def exact_dot(a, b, dims):
    return lax.dot_general(a, b, (dims, ((), ())), precision=HIGHEST, preferred_element_type=F32)


def left_lanes(rows):
    return lax.broadcasted_iota(jnp.int32, (rows, 128), 1) < 64


def rows_on(r, w):
    parts = [
        exact_dot(r[g * GROUP : (g + 1) * GROUP], w[g * ROWS : (g + 1) * ROWS].astype(F32), ((1,), (1,)))
        for g in range(2)
    ]
    return jnp.concatenate(parts, axis=1)


def choose_kernel(ring_ref, swap_ref, r_ref, w_both_ref, v_ref):
    straight = lax.axis_index("yh") == lax.axis_index("yl")
    ring, pair = ring_ref[...], swap_ref[...]
    for i, w in enumerate((jnp.where(straight, pair, ring), jnp.where(straight, ring, pair))):
        for g in range(2):
            w_both_ref[(2 * i + g) * ROWS : (2 * i + g + 1) * ROWS] = w[:, g * HD : (g + 1) * HD]
    v_ref[...] = rows_on(r_ref, w_both_ref[: 2 * ROWS])


def read_kernel(w_both_ref, own_ref, r_ref, v_ref):
    v = jnp.concatenate([own_ref[...], rows_on(r_ref, w_both_ref[2 * ROWS :])], axis=0).astype(BF16)
    for i in range(32):
        v_ref[i * 16 : (i + 1) * 16] = v


def row_sum_of_transpose(a):
    return jnp.sum(a.T, axis=0, keepdims=True)


def load_kernel(x_ref, after_ref, xv_ref, ss_ref, sem):
    copy = pltpu.make_async_copy(x_ref, xv_ref, sem)
    copy.start()
    copy.wait()
    total = jnp.zeros((xv_ref.shape[0], 128), F32)
    for b in range(xv_ref.shape[1] // 128):
        xb = xv_ref[:, b * 128 : (b + 1) * 128].astype(F32)
        total += xb * xb
    ss_ref[...] = row_sum_of_transpose(total)


def load(x, after):
    return pl.pallas_call(
        load_kernel,
        in_specs=[HBM, ANY],
        out_specs=[VMEM] * 2,
        out_shape=[shape(*x.shape, dtype=BF16), shape(1, x.shape[0])],
        scratch_shapes=[pltpu.SemaphoreType.DMA],
        compiler_params=LOADS,
    )(x, after)


def attention_kernel(q_ref, k_ref, after_ref, p_ref):
    length = q_ref.shape[0]
    rows = lax.broadcasted_iota(jnp.int32, (length, length), 0)
    cols = lax.broadcasted_iota(jnp.int32, (length, length), 1)
    allowed = cols <= rows
    for h in range(HALF):
        g = h // GROUP
        s = lax.dot_general(
            q_ref[:, h * HD : (h + 1) * HD],
            k_ref[:, g * HD : (g + 1) * HD],
            (((1,), (1,)), ((), ())),
            preferred_element_type=F32,
        )
        s = jnp.where(allowed, s * (HD**-0.5), -1e30)
        e = jnp.exp(s - jnp.max(s, axis=1, keepdims=True))
        p_ref[h] = (e / jnp.sum(e, axis=1, keepdims=True)).astype(BF16)


def attention(queries, keys, after):
    length = queries.shape[0]
    return whole(attention_kernel, shape(HALF, length, length, dtype=BF16), queries, keys, after)


def project_half(v_ref, gain_ref, x_ref, gvt_ref, core):
    low = left_lanes(8)
    total = jnp.zeros((32, x_ref.shape[0]), F32)
    for xi in range(4):
        for zp in range(4):
            row = (xi * 8 + 2 * zp) * 16
            quad = v_ref[row : row + 32].astype(F32)
            halves = []
            for h in range(2):
                one, two = quad[h * 8 : h * 8 + 8], quad[h * 8 + 16 : h * 8 + 24]
                halves.append(jnp.where(low, one, pltpu.roll(two, 64, 1)))
                halves.append(jnp.where(low, pltpu.roll(one, 64, 1), two))
            zero = (xi * 8 + zp) * 128
            gain = jnp.where(
                core == 0,
                gain_ref[:, zero : zero + 128].astype(F32),
                gain_ref[:, zero + 512 : zero + 640].astype(F32),
            )
            at = (xi * 4 + zp) * 128
            gvt_ref[:, at : at + 128] = (jnp.concatenate(halves, axis=0) * gain).astype(BF16)
        spot = pl.ds(pl.multiple_of(xi * 1024 + core * 512, 512), 512)
        total += lax.dot_general(
            gvt_ref[:, xi * 512 : (xi + 1) * 512],
            x_ref[:, spot],
            (((1,), (1,)), ((), ())),
            preferred_element_type=F32,
        )
    return total


def project_own_kernel(v_ref, gain_ref, x_ref, gvt_ref, u_ref):
    u_ref[...] = project_half(v_ref, gain_ref, x_ref, gvt_ref, lax.axis_index("core"))


def project_got_kernel(v_ref, gain_ref, x_ref, part_ref, ss_ref, gvt_ref, u_ref, send_ref):
    u = part_ref[...] + project_half(v_ref, gain_ref, x_ref, gvt_ref, 1 - lax.axis_index("core"))
    u_ref[...] = u[:HALF]
    send_ref[:HALF] = u[HALF:]
    send_ref[HALF:] = jnp.broadcast_to(ss_ref[...], (8, u.shape[1]))


def project(own, got, gain, x, ss):
    length, wide = x.shape
    half = shape(32, wide // 2, dtype=BF16)
    mine, part = whole(project_own_kernel, [half, shape(32, length)], own, gain, x)
    other, u, send = whole(
        project_got_kernel,
        [half, shape(HALF, length), shape(HALF + 8, length)],
        got, gain, x, part, ss,
    )
    return (mine, other), u, send


def values_kernel(width, p_ref, own_ref, got_ref, ss_ref, v_ref, u_ref, rms_ref):
    got = got_ref[...]
    rms = lax.rsqrt((ss_ref[...] + got[HALF : HALF + 1]) / width + EPS)
    rms_ref[...] = rms
    u = own_ref[...] + got[:HALF]
    u_ref[...] = u
    u = u * rms
    total = jnp.zeros(p_ref.shape[1:], F32)
    for j in range(HALF):
        total += p_ref[j].astype(F32) * u[j : j + 1]
    v_ref[...] = row_sum_of_transpose(total)


def make_values(width, probs, own, got, ss):
    length = probs.shape[1]
    return whole(
        lambda *refs: values_kernel(width, *refs),
        [shape(1, length), shape(HALF, length), shape(1, length)],
        probs, own, got, ss,
    )


def error_kernel(p_ref, u_ref, own_ref, got_ref, targets_ref, scored_ref, values_ref, c_ref):
    length = u_ref.shape[1]
    values = own_ref[...] + got_ref[...]
    values_ref[...] = values
    error = (values - targets_ref[...]) * scored_ref[...].astype(F32)
    high = error.astype(BF16)
    low = (error - high.astype(F32)).astype(BF16)
    both = jnp.concatenate([jnp.broadcast_to(high, (8, length)), jnp.broadcast_to(low, (8, length))], axis=0)
    rows = []
    for j in range(HALF):
        c = jnp.dot(both, p_ref[j], preferred_element_type=F32)
        rows.append(c[:1] + c[8:9])
    c = jnp.concatenate(rows, axis=0)
    c_ref[:HALF] = c
    c_ref[HALF:] = jnp.broadcast_to(jnp.sum(c * u_ref[...], axis=0, keepdims=True), (8, length))


def make_error(probs, u, own, got, targets, scored):
    length = probs.shape[1]
    return whole(
        error_kernel, [shape(1, length), shape(HALF + 8, length)], probs, u, own, got, targets, scored
    )


def rows_kernel(own_ref, got_ref, rms_ref, x_ref, c_ref, dot_ref, keep_ref, send_ref):
    core = lax.axis_index("core")
    c = jnp.concatenate([own_ref[:HALF], got_ref[:HALF]], axis=0) * rms_ref[...]
    c_ref[...] = c
    dot_ref[...] = own_ref[HALF : HALF + 1] + got_ref[HALF : HALF + 1]
    high = c.astype(BF16)
    low = (c - high.astype(F32)).astype(BF16)
    both = jnp.concatenate([high, low], axis=0)
    z = jnp.dot(both, x_ref[...], preferred_element_type=F32)
    z = z[:32] + z[32:]
    left = left_lanes(8)

    def chunks(b):
        at = slice(b * 128, (b + 1) * 128)
        parts = [z[i * 8 : (i + 1) * 8, at] for i in range(4)]
        even = [jnp.where(left, parts[i], pltpu.roll(parts[i + 1], 64, 1)) for i in (0, 2)]
        odd = [jnp.where(left, pltpu.roll(parts[i], 64, 1), parts[i + 1]) for i in (0, 2)]
        return jnp.concatenate([*even, *odd], axis=0)

    for xi in range(4):
        for zp in range(4):
            at = pl.ds((xi * 4 + zp) * 32, 32)
            zero, one = chunks(xi * 8 + zp), chunks(xi * 8 + 4 + zp)
            keep_ref[at] = jnp.where(core == 0, zero, one)
            send_ref[at] = jnp.where(core == 0, one, zero).astype(BF16)


def make_rows(own, got, rms, x):
    length = x.shape[0]
    return whole(
        rows_kernel,
        [shape(32, length), shape(1, length), shape(512, 128), shape(512, 128, dtype=BF16)],
        own, got, rms, x,
    )


def sum_kernel(parts_ref, gain_ref, v_ref, w_ref, tails_ref):
    side = lax.axis_index("yl")
    xi, zi = lax.axis_index("x"), lax.axis_index("z")
    even = zi % 2 == 0
    v = v_ref[pl.ds(pl.multiple_of((xi * 8 + zi) * 16, 16), 16)].astype(F32)
    spot = (xi * 2 + lax.axis_index("core")) * 4 + zi // 2
    gain = jnp.zeros((1, 128), F32)
    for b in range(BLOCKS // 2):
        gain = jnp.where(spot == b, gain_ref[:, b * 128 : (b + 1) * 128].astype(F32), gain)
    gain = jnp.where(left_lanes(1) == even, gain, pltpu.roll(gain, 64, 1))
    total = jnp.zeros((HALF, 128), F32)
    for b in range(32):
        total += parts_ref[b].astype(F32)
    z = total * gain
    part = jnp.sum(total * v, axis=0, keepdims=True)
    part = jnp.broadcast_to(part + pltpu.roll(part, 64, 1), (8, 128))
    ws = [w_ref[i * ROWS : (i + 1) * ROWS].astype(F32) for i in range(4)]
    tails = []
    for h in range(2):
        rows = z[h * 8 : (h + 1) * 8]
        reads = []
        for g in range(2):
            reads.append(exact_dot(rows[:, g * ROWS : (g + 1) * ROWS], ws[2 * h + g], ((1,), (0,))))
        tails.append(jnp.concatenate([*reads, part, rows], axis=0))
    for i in range(8):
        tails_ref[i] = jnp.where(side == i % 2, tails[0], tails[1]).astype(BF16)


def weight_kernel(z_ref, r_ref, grad_ref):
    for g in range(2):
        z = z_ref[:, g * ROWS : (g + 1) * ROWS]
        grad_ref[:, g * HD : (g + 1) * HD] = exact_dot(z, r_ref[g * GROUP : (g + 1) * GROUP], ((0,), (0,)))


def near_kernel(tails_ref, out_ref, z_ref):
    core, side, far = lax.axis_index("core"), lax.axis_index("yl"), lax.axis_index("yh")
    read = tails_ref[0].astype(F32)[:HALF]
    for i in range(1, 8):
        read += tails_ref[i].astype(F32)[:HALF]

    def pair(i):
        return tails_ref[i].astype(F32) + tails_ref[4 + i].astype(F32)

    zero, one = pair(side)[HALF : HALF + 8], pair(2 + side)[HALF : HALF + 8]
    z_ref[...] = pair(2 * core + far)[HALF + 8 :]
    tail = jnp.concatenate([read, jnp.where(left_lanes(8), zero, one)], axis=0).astype(BF16)
    for i in range(32):
        out_ref[i] = tail


def last_kernel(all_ref, read_ref, gain_ref):
    left = left_lanes(1)
    total = all_ref[0].astype(F32)
    for i in range(1, 32):
        total += all_ref[i].astype(F32)
    read_ref[...] = total[:HALF]
    for xi in range(4):
        for zp in range(4):
            i = xi * 8 + 2 * zp
            one = all_ref[i].astype(F32)[HALF : HALF + 1]
            two = all_ref[i + 1].astype(F32)[HALF : HALF + 1]
            row = xi * 8 + zp
            gain_ref[row : row + 1] = jnp.where(left, one, pltpu.roll(two, 64, 1))
            gain_ref[row + 4 : row + 5] = jnp.where(left, pltpu.roll(one, 64, 1), two)


def input_kernel(width, c_ref, dot_ref, rms_ref, mine_ref, other_ref, x_ref, after_ref, out_ref, log_ref):
    rms = rms_ref[...]
    length = rms.shape[1]
    c = c_ref[...]
    high = c.astype(BF16)
    low = (c - high.astype(F32)).astype(BF16)
    log_scale = rms * dot_ref[...]
    log_ref[...] = log_scale
    back = jnp.broadcast_to(rms * rms * log_scale / width, (128, length)).T
    first = lax.axis_index("core") == 0
    mine, other = mine_ref[...], other_ref[...]
    gvt = jnp.concatenate([jnp.where(first, mine, other), jnp.where(first, other, mine)], axis=1)
    grad = lax.dot_general(
        jnp.concatenate([high, low], axis=0),
        jnp.concatenate([gvt, gvt], axis=0),
        (((0,), (0,)), ((), ())),
        preferred_element_type=F32,
    )
    for b in range(grad.shape[1] // 128):
        at = slice(b * 128, (b + 1) * 128)
        out_ref[:, at] = (grad[:, at] - x_ref[:, at].astype(F32) * back).astype(BF16)


def input_grad(width, c, dot, rms, gvt, x, after):
    steps = 4
    length, wide = x.shape
    return pl.pallas_call(
        lambda *refs: input_kernel(width, *refs),
        grid=(steps,),
        in_specs=[
            pl.BlockSpec((32, length), lambda i: (0, 0)),
            pl.BlockSpec((1, length), lambda i: (0, 0)),
            pl.BlockSpec((1, length), lambda i: (0, 0)),
            pl.BlockSpec((32, wide // steps // 2), lambda i: (0, i)),
            pl.BlockSpec((32, wide // steps // 2), lambda i: (0, i)),
            pl.BlockSpec((length, wide // steps), lambda i: (0, i)),
            ANY,
        ],
        out_specs=[
            pl.BlockSpec((length, wide // steps), lambda i: (0, i)),
            pl.BlockSpec((1, length), lambda i: (0, 0)),
        ],
        out_shape=[shape(length, wide, dtype=BF16), shape(1, length)],
        compiler_params=PARAMS,
    )(c, dot, rms, *gvt, x, after)


def together(*values):
    return lax.optimization_barrier(values)


def shards(hidden_states, norm_gain, value_weight, queries, keys, readout, targets, scored):
    width = hidden_states.shape[1] * 2
    read = readout.reshape(HALF, HD)
    other_read = swap(read, "yl")
    ring = lax.ppermute(value_weight, ("yh", "yl"), [(1, 0), (0, 2), (2, 3), (3, 1)])
    pair = cross(value_weight)
    x, ss = load(hidden_states, norm_gain)
    ring, pair, ss = together(ring, pair, ss)
    weight, v = whole(
        choose_kernel, [shape(256, 128, dtype=BF16), shape(8, 128)], ring, pair, read
    )
    v, other_read = together(v, other_read)
    v = whole(read_kernel, shape(512, 128, dtype=BF16), weight, v, other_read)
    v = lax.all_to_all(v.reshape(32, HALF, 128), PLANE, 0, 0).reshape(512, 128)
    v, norm_gain, targets, scored = together(v, norm_gain, targets, scored)
    gain = norm_gain[None]
    gvt, u, send = project(v, swap(v, "core"), gain, x, ss)
    probs = attention(queries, keys, u)
    part, u, rms = make_values(width, probs, u, swap(send, "yl"), ss)
    got = swap(part, "yl")
    values, c = make_error(probs, u, part, got, targets[None], scored[None])
    c, dot, keep, send = make_rows(c, swap(c, "yl"), rms, x)
    z = (keep + swap(send, "core").astype(F32)).astype(BF16).reshape(32, HALF, 128)
    z = lax.all_to_all(z, PLANE, 0, 0)
    grad_input, log_scale = input_grad(width, c, dot, rms, gvt, x, z)
    tails = whole(sum_kernel, shape(8, HALF + 16, 128, dtype=BF16), z, gain, v, weight)
    tails = lax.all_to_all(tails, NEAR, 0, 0)
    tails, z = whole(near_kernel, [shape(32, HALF + 8, 128, dtype=BF16), shape(8, 128)], tails)
    grad_weight = whole(weight_kernel, shape(ROWS, 2 * HD), z, read)
    tails = lax.all_to_all(tails, PLANE, 0, 0)
    grad_readout, grad_gain = whole(last_kernel, [shape(HALF, HD), shape(32, 128)], tails)
    return (values[0], grad_input, grad_weight, grad_gain.reshape(-1), grad_readout.reshape(-1), log_scale[0])


def solution(mesh):
    fine = Mesh(mesh.devices.reshape(2, 4, 2, 8, 2), ("yh", "x", "core", "z", "yl"))
    seq = ("yh", "x", "core", "z")
    return jax.shard_map(
        shards,
        mesh=fine,
        in_specs=(
            P(seq, "yl"),
            P("yl"),
            P(seq, "yl"),
            P(seq, "yl"),
            P(seq, "yl"),
            P("yl"),
            P(seq),
            P(seq),
        ),
        out_specs=(
            P(seq),
            P(seq, "yl"),
            P(seq, "yl"),
            P("yl"),
            P("yl"),
            P(seq),
        ),
        check_vma=False,
    )
```

```python
import jax
import jax.numpy as jnp
from jax import lax
from jax.experimental import pallas as pl
from jax.experimental.pallas import tpu as pltpu
from jax.sharding import Mesh
from jax.sharding import PartitionSpec as P

HD = 128
GROUP = 8
EPS = 1e-06
F32 = jnp.float32
BF16 = jnp.bfloat16
HIGHEST = lax.Precision.HIGHEST
VMEM = pl.BlockSpec(memory_space=pltpu.VMEM)
HBM = pl.BlockSpec(memory_space=pltpu.HBM)
ANY = pl.BlockSpec(memory_space=pl.ANY)
LOADS = pltpu.CompilerParams(vmem_limit_bytes=51 * 1024 * 1024)
PARAMS = pltpu.CompilerParams(vmem_limit_bytes=16 * 1024 * 1024)


PLANE = ("x", "z")
NEAR = ("yh", "core", "yl")
ROWS = 64
BLOCKS = 64
HALF = 16


def swap(v, axis):
    return lax.ppermute(v, axis, [(0, 1), (1, 0)])


def cross(v):
    return lax.ppermute(v, ("yh", "yl"), [(0, 0), (1, 2), (2, 1), (3, 3)])


def split(bit, v, axis):
    n = v.shape[axis] // 2
    low = lax.slice_in_dim(v, 0, n, axis=axis)
    high = lax.slice_in_dim(v, n, 2 * n, axis=axis)
    return jnp.where(bit, high, low), jnp.where(bit, low, high)


def whole(body, out_shape, *args, scratch=()):
    many = isinstance(out_shape, list)
    return pl.pallas_call(
        body,
        in_specs=[VMEM] * len(args),
        out_specs=[VMEM] * len(out_shape) if many else VMEM,
        out_shape=out_shape,
        scratch_shapes=scratch,
        compiler_params=PARAMS,
    )(*args)


def shape(*dims, dtype=F32):
    return jax.ShapeDtypeStruct(dims, dtype)


def exact_dot(a, b, dims):
    return lax.dot_general(a, b, (dims, ((), ())), precision=HIGHEST, preferred_element_type=F32)


def split_dot(a, w, dims):
    high = a.astype(BF16)
    low = (a - high.astype(F32)).astype(BF16)
    both = jnp.concatenate([high.astype(F32), low.astype(F32)], axis=0).astype(BF16)
    out = lax.dot_general(both, w, (dims, ((), ())), preferred_element_type=F32)
    return out[: a.shape[0]] + out[a.shape[0] :]


def left_lanes(rows):
    return lax.broadcasted_iota(jnp.int32, (rows, 128), 1) < 64


def rows_on(r, w):
    parts = [
        split_dot(r[g * GROUP : (g + 1) * GROUP], w[g * ROWS : (g + 1) * ROWS], ((1,), (1,)))
        for g in range(2)
    ]
    return jnp.concatenate(parts, axis=1)


def choose_kernel(ring_ref, swap_ref, r_ref, w_both_ref, v_ref):
    straight = lax.axis_index("yh") == lax.axis_index("yl")
    ring, pair = ring_ref[...], swap_ref[...]
    for i, w in enumerate((jnp.where(straight, pair, ring), jnp.where(straight, ring, pair))):
        for g in range(2):
            w_both_ref[(2 * i + g) * ROWS : (2 * i + g + 1) * ROWS] = w[:, g * HD : (g + 1) * HD]
    v_ref[...] = rows_on(r_ref, w_both_ref[: 2 * ROWS])


def read_kernel(w_both_ref, own_ref, r_ref, v_ref):
    v = jnp.concatenate([own_ref[...], rows_on(r_ref, w_both_ref[2 * ROWS :])], axis=0).astype(BF16)
    for i in range(32):
        v_ref[i * 16 : (i + 1) * 16] = v


def row_sum_of_transpose(a):
    return jnp.sum(a.T, axis=0, keepdims=True)


def load_kernel(x_ref, after_ref, xv_ref, ss_ref, sems):
    wide = xv_ref.shape[1]
    spots = [slice(i * wide // 4, (i + 1) * wide // 4) for i in range(4)]
    copies = [pltpu.make_async_copy(x_ref.at[:, s], xv_ref.at[:, s], sems.at[i]) for i, s in enumerate(spots)]
    for copy in copies:
        copy.start()
    total = jnp.zeros((xv_ref.shape[0], 128), F32)
    for copy, spot in zip(copies, spots):
        copy.wait()
        for at in range(spot.start, spot.stop, 128):
            xb = xv_ref[:, at : at + 128].astype(F32)
            total += xb * xb
    ss_ref[...] = row_sum_of_transpose(total)


def load(x, after):
    return pl.pallas_call(
        load_kernel,
        in_specs=[HBM, ANY],
        out_specs=[VMEM] * 2,
        out_shape=[shape(*x.shape, dtype=BF16), shape(1, x.shape[0])],
        scratch_shapes=[pltpu.SemaphoreType.DMA((4,))],
        compiler_params=LOADS,
    )(x, after)


def attention_kernel(q_ref, k_ref, after_ref, p_ref):
    length = q_ref.shape[0]
    rows = lax.broadcasted_iota(jnp.int32, (length, length), 0)
    cols = lax.broadcasted_iota(jnp.int32, (length, length), 1)
    allowed = cols <= rows
    for h in range(HALF):
        g = h // GROUP
        s = lax.dot_general(
            q_ref[:, h * HD : (h + 1) * HD],
            k_ref[:, g * HD : (g + 1) * HD],
            (((1,), (1,)), ((), ())),
            preferred_element_type=F32,
        )
        s = jnp.where(allowed, s * (HD**-0.5), -1e30)
        e = jnp.exp(s - jnp.max(s, axis=1, keepdims=True))
        p_ref[h] = (e / jnp.sum(e, axis=1, keepdims=True)).astype(BF16)


def attention(queries, keys, after):
    length = queries.shape[0]
    return whole(attention_kernel, shape(HALF, length, length, dtype=BF16), queries, keys, after)


def project_half(v_ref, gain_ref, x_ref, gvt_ref, core):
    low = left_lanes(8)
    total = jnp.zeros((32, x_ref.shape[0]), F32)
    for xi in range(4):
        for zp in range(4):
            row = (xi * 8 + 2 * zp) * 16
            quad = v_ref[row : row + 32].astype(F32)
            halves = []
            for h in range(2):
                one, two = quad[h * 8 : h * 8 + 8], quad[h * 8 + 16 : h * 8 + 24]
                halves.append(jnp.where(low, one, pltpu.roll(two, 64, 1)))
                halves.append(jnp.where(low, pltpu.roll(one, 64, 1), two))
            zero = (xi * 8 + zp) * 128
            gain = jnp.where(
                core == 0,
                gain_ref[:, zero : zero + 128].astype(F32),
                gain_ref[:, zero + 512 : zero + 640].astype(F32),
            )
            at = (xi * 4 + zp) * 128
            gvt_ref[:, at : at + 128] = (jnp.concatenate(halves, axis=0) * gain).astype(BF16)
        spot = pl.ds(pl.multiple_of(xi * 1024 + core * 512, 512), 512)
        total += lax.dot_general(
            gvt_ref[:, xi * 512 : (xi + 1) * 512],
            x_ref[:, spot],
            (((1,), (1,)), ((), ())),
            preferred_element_type=F32,
        )
    return total


def project_own_kernel(v_ref, gain_ref, x_ref, gvt_ref, u_ref):
    u_ref[...] = project_half(v_ref, gain_ref, x_ref, gvt_ref, lax.axis_index("core"))


def project_got_kernel(v_ref, gain_ref, x_ref, part_ref, ss_ref, gvt_ref, u_ref, send_ref):
    u = part_ref[...] + project_half(v_ref, gain_ref, x_ref, gvt_ref, 1 - lax.axis_index("core"))
    u_ref[...] = u[:HALF]
    send_ref[:HALF] = u[HALF:]
    send_ref[HALF:] = jnp.broadcast_to(ss_ref[...], (8, u.shape[1]))


def project(own, got, gain, x, ss):
    length, wide = x.shape
    half = shape(32, wide // 2, dtype=BF16)
    mine, part = whole(project_own_kernel, [half, shape(32, length)], own, gain, x)
    other, u, send = whole(
        project_got_kernel,
        [half, shape(HALF, length), shape(HALF + 8, length)],
        got, gain, x, part, ss,
    )
    return (mine, other), u, send


def values_kernel(width, p_ref, own_ref, got_ref, ss_ref, v_ref, u_ref, rms_ref):
    got = got_ref[...]
    rms = lax.rsqrt((ss_ref[...] + got[HALF : HALF + 1]) / width + EPS)
    rms_ref[...] = rms
    u = own_ref[...] + got[:HALF]
    u_ref[...] = u
    u = u * rms
    total = jnp.zeros(p_ref.shape[1:], F32)
    for j in range(HALF):
        total += p_ref[j].astype(F32) * u[j : j + 1]
    v_ref[...] = row_sum_of_transpose(total)


def make_values(width, probs, own, got, ss):
    length = probs.shape[1]
    return whole(
        lambda *refs: values_kernel(width, *refs),
        [shape(1, length), shape(HALF, length), shape(1, length)],
        probs, own, got, ss,
    )


def error_kernel(p_ref, u_ref, own_ref, got_ref, targets_ref, scored_ref, values_ref, c_ref):
    length = u_ref.shape[1]
    values = own_ref[...] + got_ref[...]
    values_ref[...] = values
    error = (values - targets_ref[...]) * scored_ref[...].astype(F32)
    high = error.astype(BF16)
    low = (error - high.astype(F32)).astype(BF16)
    both = jnp.concatenate([jnp.broadcast_to(high, (8, length)), jnp.broadcast_to(low, (8, length))], axis=0)
    rows = []
    for j in range(HALF):
        c = jnp.dot(both, p_ref[j], preferred_element_type=F32)
        rows.append(c[:1] + c[8:9])
    c = jnp.concatenate(rows, axis=0)
    c_ref[:HALF] = c
    c_ref[HALF:] = jnp.broadcast_to(jnp.sum(c * u_ref[...], axis=0, keepdims=True), (8, length))


def make_error(probs, u, own, got, targets, scored):
    length = probs.shape[1]
    return whole(
        error_kernel, [shape(1, length), shape(HALF + 8, length)], probs, u, own, got, targets, scored
    )


def rows_kernel(own_ref, got_ref, rms_ref, x_ref, c_ref, dot_ref, keep_ref, send_ref):
    core = lax.axis_index("core")
    c = jnp.concatenate([own_ref[:HALF], got_ref[:HALF]], axis=0) * rms_ref[...]
    c_ref[...] = c
    dot_ref[...] = own_ref[HALF : HALF + 1] + got_ref[HALF : HALF + 1]
    high = c.astype(BF16)
    low = (c - high.astype(F32)).astype(BF16)
    both = jnp.concatenate([high, low], axis=0)
    z = jnp.dot(both, x_ref[...], preferred_element_type=F32)
    z = z[:32] + z[32:]
    left = left_lanes(8)

    def chunks(b):
        at = slice(b * 128, (b + 1) * 128)
        parts = [z[i * 8 : (i + 1) * 8, at] for i in range(4)]
        even = [jnp.where(left, parts[i], pltpu.roll(parts[i + 1], 64, 1)) for i in (0, 2)]
        odd = [jnp.where(left, pltpu.roll(parts[i], 64, 1), parts[i + 1]) for i in (0, 2)]
        return jnp.concatenate([*even, *odd], axis=0)

    for xi in range(4):
        for zp in range(4):
            at = pl.ds((xi * 4 + zp) * 32, 32)
            zero, one = chunks(xi * 8 + zp), chunks(xi * 8 + 4 + zp)
            keep_ref[at] = jnp.where(core == 0, zero, one)
            send_ref[at] = jnp.where(core == 0, one, zero).astype(BF16)


def make_rows(own, got, rms, x):
    length = x.shape[0]
    return whole(
        rows_kernel,
        [shape(32, length), shape(1, length), shape(512, 128), shape(512, 128, dtype=BF16)],
        own, got, rms, x,
    )


def sum_kernel(parts_ref, gain_ref, v_ref, w_ref, tails_ref):
    side = lax.axis_index("yl")
    xi, zi = lax.axis_index("x"), lax.axis_index("z")
    even = zi % 2 == 0
    v = v_ref[pl.ds(pl.multiple_of((xi * 8 + zi) * 16, 16), 16)].astype(F32)
    spot = (xi * 2 + lax.axis_index("core")) * 4 + zi // 2
    gain = jnp.zeros((1, 128), F32)
    for b in range(BLOCKS // 2):
        gain = jnp.where(spot == b, gain_ref[:, b * 128 : (b + 1) * 128].astype(F32), gain)
    gain = jnp.where(left_lanes(1) == even, gain, pltpu.roll(gain, 64, 1))
    total = jnp.zeros((HALF, 128), F32)
    for b in range(32):
        total += parts_ref[b].astype(F32)
    z = total * gain
    part = jnp.sum(total * v, axis=0, keepdims=True)
    part = jnp.broadcast_to(part + pltpu.roll(part, 64, 1), (8, 128))
    ws = [w_ref[i * ROWS : (i + 1) * ROWS] for i in range(4)]
    tails = []
    for h in range(2):
        rows = z[h * 8 : (h + 1) * 8]
        reads = []
        for g in range(2):
            reads.append(split_dot(rows[:, g * ROWS : (g + 1) * ROWS], ws[2 * h + g], ((1,), (0,))))
        tails.append(jnp.concatenate([*reads, part, rows], axis=0))
    for i in range(8):
        tails_ref[i] = jnp.where(side == i % 2, tails[0], tails[1]).astype(BF16)


def weight_kernel(z_ref, r_ref, grad_ref):
    for g in range(2):
        z = z_ref[:, g * ROWS : (g + 1) * ROWS]
        grad_ref[:, g * HD : (g + 1) * HD] = exact_dot(z, r_ref[g * GROUP : (g + 1) * GROUP], ((0,), (0,)))


def near_kernel(tails_ref, out_ref, z_ref):
    core, side, far = lax.axis_index("core"), lax.axis_index("yl"), lax.axis_index("yh")
    read = tails_ref[0].astype(F32)[:HALF]
    for i in range(1, 8):
        read += tails_ref[i].astype(F32)[:HALF]

    def pair(i):
        return tails_ref[i].astype(F32) + tails_ref[4 + i].astype(F32)

    zero, one = pair(side)[HALF : HALF + 8], pair(2 + side)[HALF : HALF + 8]
    z_ref[...] = pair(2 * core + far)[HALF + 8 :]
    tail = jnp.concatenate([read, jnp.where(left_lanes(8), zero, one)], axis=0).astype(BF16)
    for i in range(32):
        out_ref[i] = tail


def last_kernel(all_ref, read_ref, gain_ref):
    left = left_lanes(1)
    total = all_ref[0].astype(F32)
    for i in range(1, 32):
        total += all_ref[i].astype(F32)
    read_ref[...] = total[:HALF]
    for xi in range(4):
        for zp in range(4):
            i = xi * 8 + 2 * zp
            one = all_ref[i].astype(F32)[HALF : HALF + 1]
            two = all_ref[i + 1].astype(F32)[HALF : HALF + 1]
            row = xi * 8 + zp
            gain_ref[row : row + 1] = jnp.where(left, one, pltpu.roll(two, 64, 1))
            gain_ref[row + 4 : row + 5] = jnp.where(left, pltpu.roll(one, 64, 1), two)


def input_kernel(width, c_ref, dot_ref, rms_ref, mine_ref, other_ref, x_ref, after_ref, out_ref, log_ref):
    rms = rms_ref[...]
    length = rms.shape[1]
    c = c_ref[...]
    high = c.astype(BF16)
    low = (c - high.astype(F32)).astype(BF16)
    log_scale = rms * dot_ref[...]
    log_ref[...] = log_scale
    back = jnp.broadcast_to(rms * rms * log_scale / width, (128, length)).T
    first = lax.axis_index("core") == 0
    mine, other = mine_ref[...], other_ref[...]
    gvt = jnp.concatenate([jnp.where(first, mine, other), jnp.where(first, other, mine)], axis=1)
    grad = lax.dot_general(
        jnp.concatenate([high, low], axis=0),
        jnp.concatenate([gvt, gvt], axis=0),
        (((0,), (0,)), ((), ())),
        preferred_element_type=F32,
    )
    for b in range(grad.shape[1] // 128):
        at = slice(b * 128, (b + 1) * 128)
        out_ref[:, at] = (grad[:, at] - x_ref[:, at].astype(F32) * back).astype(BF16)


def input_grad(width, c, dot, rms, gvt, x, after):
    steps = 4
    length, wide = x.shape
    return pl.pallas_call(
        lambda *refs: input_kernel(width, *refs),
        grid=(steps,),
        in_specs=[
            pl.BlockSpec((32, length), lambda i: (0, 0)),
            pl.BlockSpec((1, length), lambda i: (0, 0)),
            pl.BlockSpec((1, length), lambda i: (0, 0)),
            pl.BlockSpec((32, wide // steps // 2), lambda i: (0, i)),
            pl.BlockSpec((32, wide // steps // 2), lambda i: (0, i)),
            pl.BlockSpec((length, wide // steps), lambda i: (0, i)),
            ANY,
        ],
        out_specs=[
            pl.BlockSpec((length, wide // steps), lambda i: (0, i)),
            pl.BlockSpec((1, length), lambda i: (0, 0)),
        ],
        out_shape=[shape(length, wide, dtype=BF16), shape(1, length)],
        compiler_params=PARAMS,
    )(c, dot, rms, *gvt, x, after)


def together(*values):
    return lax.optimization_barrier(values)


def shards(hidden_states, norm_gain, value_weight, queries, keys, readout, targets, scored):
    width = hidden_states.shape[1] * 2
    read = readout.reshape(HALF, HD)
    other_read = swap(read, "yl")
    ring = lax.ppermute(value_weight, ("yh", "yl"), [(1, 0), (0, 2), (2, 3), (3, 1)])
    pair = cross(value_weight)
    x, ss = load(hidden_states, norm_gain)
    ring, pair, ss = together(ring, pair, ss)
    weight, v = whole(
        choose_kernel, [shape(256, 128, dtype=BF16), shape(8, 128)], ring, pair, read
    )
    v, other_read = together(v, other_read)
    v = whole(read_kernel, shape(512, 128, dtype=BF16), weight, v, other_read)
    v = lax.all_to_all(v.reshape(32, HALF, 128), PLANE, 0, 0).reshape(512, 128)
    v, norm_gain, targets, scored = together(v, norm_gain, targets, scored)
    gain = norm_gain[None]
    gvt, u, send = project(v, swap(v, "core"), gain, x, ss)
    probs = attention(queries, keys, u)
    part, u, rms = make_values(width, probs, u, swap(send, "yl"), ss)
    got = swap(part, "yl")
    values, c = make_error(probs, u, part, got, targets[None], scored[None])
    c, dot, keep, send = make_rows(c, swap(c, "yl"), rms, x)
    z = (keep + swap(send, "core").astype(F32)).astype(BF16).reshape(32, HALF, 128)
    z = lax.all_to_all(z, PLANE, 0, 0)
    grad_input, log_scale = input_grad(width, c, dot, rms, gvt, x, z)
    tails = whole(sum_kernel, shape(8, HALF + 16, 128, dtype=BF16), z, gain, v, weight)
    tails = lax.all_to_all(tails, NEAR, 0, 0)
    tails, z = whole(near_kernel, [shape(32, HALF + 8, 128, dtype=BF16), shape(8, 128)], tails)
    grad_weight = whole(weight_kernel, shape(ROWS, 2 * HD), z, read)
    tails = lax.all_to_all(tails, PLANE, 0, 0)
    grad_readout, grad_gain = whole(last_kernel, [shape(HALF, HD), shape(32, 128)], tails)
    return (values[0], grad_input, grad_weight, grad_gain.reshape(-1), grad_readout.reshape(-1), log_scale[0])


def solution(mesh):
    fine = Mesh(mesh.devices.reshape(2, 4, 2, 8, 2), ("yh", "x", "core", "z", "yl"))
    seq = ("yh", "x", "core", "z")
    return jax.shard_map(
        shards,
        mesh=fine,
        in_specs=(
            P(seq, "yl"),
            P("yl"),
            P(seq, "yl"),
            P(seq, "yl"),
            P(seq, "yl"),
            P("yl"),
            P(seq),
            P(seq),
        ),
        out_specs=(
            P(seq),
            P(seq, "yl"),
            P(seq, "yl"),
            P("yl"),
            P("yl"),
            P(seq),
        ),
        check_vma=False,
    )
```

```python
import jax
import jax.numpy as jnp
from jax import lax
from jax.experimental import pallas as pl
from jax.experimental.pallas import tpu as pltpu
from jax.sharding import Mesh
from jax.sharding import PartitionSpec as P

HD = 128
GROUP = 8
EPS = 1e-06
F32 = jnp.float32
BF16 = jnp.bfloat16
HIGHEST = lax.Precision.HIGHEST
VMEM = pl.BlockSpec(memory_space=pltpu.VMEM)
HBM = pl.BlockSpec(memory_space=pltpu.HBM)
ANY = pl.BlockSpec(memory_space=pl.ANY)
LOADS = pltpu.CompilerParams(vmem_limit_bytes=51 * 1024 * 1024)
PARAMS = pltpu.CompilerParams(vmem_limit_bytes=16 * 1024 * 1024)


PLANE = ("x", "z")
NEAR = ("yh", "core", "yl")
ROWS = 64
BLOCKS = 64
HALF = 16


def swap(v, axis):
    return lax.ppermute(v, axis, [(0, 1), (1, 0)])


def cross(v):
    return lax.ppermute(v, ("yh", "yl"), [(0, 0), (1, 2), (2, 1), (3, 3)])


def split(bit, v, axis):
    n = v.shape[axis] // 2
    low = lax.slice_in_dim(v, 0, n, axis=axis)
    high = lax.slice_in_dim(v, n, 2 * n, axis=axis)
    return jnp.where(bit, high, low), jnp.where(bit, low, high)


def whole(body, out_shape, *args, scratch=()):
    many = isinstance(out_shape, list)
    return pl.pallas_call(
        body,
        in_specs=[VMEM] * len(args),
        out_specs=[VMEM] * len(out_shape) if many else VMEM,
        out_shape=out_shape,
        scratch_shapes=scratch,
        compiler_params=PARAMS,
    )(*args)


def shape(*dims, dtype=F32):
    return jax.ShapeDtypeStruct(dims, dtype)


def exact_dot(a, b, dims):
    return lax.dot_general(a, b, (dims, ((), ())), precision=HIGHEST, preferred_element_type=F32)


def split_dot(a, w, dims):
    high = a.astype(BF16)
    low = (a - high.astype(F32)).astype(BF16)
    both = jnp.concatenate([high.astype(F32), low.astype(F32)], axis=0).astype(BF16)
    out = lax.dot_general(both, w, (dims, ((), ())), preferred_element_type=F32)
    return out[: a.shape[0]] + out[a.shape[0] :]


def left_lanes(rows):
    return lax.broadcasted_iota(jnp.int32, (rows, 128), 1) < 64


def rows_on(r, w):
    parts = [
        split_dot(r[g * GROUP : (g + 1) * GROUP], w[g * ROWS : (g + 1) * ROWS], ((1,), (1,)))
        for g in range(2)
    ]
    return jnp.concatenate(parts, axis=1)


def choose_kernel(ring_ref, swap_ref, r_ref, w_both_ref, v_ref):
    straight = lax.axis_index("yh") == lax.axis_index("yl")
    ring, pair = ring_ref[...], swap_ref[...]
    for i, w in enumerate((jnp.where(straight, pair, ring), jnp.where(straight, ring, pair))):
        for g in range(2):
            w_both_ref[(2 * i + g) * ROWS : (2 * i + g + 1) * ROWS] = w[:, g * HD : (g + 1) * HD]
    v_ref[...] = rows_on(r_ref, w_both_ref[: 2 * ROWS])


def read_kernel(w_both_ref, own_ref, r_ref, v_ref):
    v = jnp.concatenate([own_ref[...], rows_on(r_ref, w_both_ref[2 * ROWS :])], axis=0).astype(BF16)
    for i in range(32):
        v_ref[i * 16 : (i + 1) * 16] = v


def row_sum_of_transpose(a):
    return jnp.sum(a.T, axis=0, keepdims=True)


def load_kernel(x_ref, after_ref, xv_ref, ss_ref, sems):
    wide = xv_ref.shape[1]
    spots = [slice(i * wide // 4, (i + 1) * wide // 4) for i in range(4)]
    copies = [pltpu.make_async_copy(x_ref.at[:, s], xv_ref.at[:, s], sems.at[i]) for i, s in enumerate(spots)]
    for copy in copies:
        copy.start()
    total = jnp.zeros((xv_ref.shape[0], 128), F32)
    for copy, spot in zip(copies, spots):
        copy.wait()
        for at in range(spot.start, spot.stop, 128):
            xb = xv_ref[:, at : at + 128].astype(F32)
            total += xb * xb
    ss_ref[...] = row_sum_of_transpose(total)


def load(x, after):
    return pl.pallas_call(
        load_kernel,
        in_specs=[HBM, ANY],
        out_specs=[VMEM] * 2,
        out_shape=[shape(*x.shape, dtype=BF16), shape(1, x.shape[0])],
        scratch_shapes=[pltpu.SemaphoreType.DMA((4,))],
        compiler_params=LOADS,
    )(x, after)


def attention_kernel(q_ref, k_ref, after_ref, p_ref):
    length = q_ref.shape[0]
    rows = lax.broadcasted_iota(jnp.int32, (length, length), 0)
    cols = lax.broadcasted_iota(jnp.int32, (length, length), 1)
    allowed = cols <= rows
    for h in range(HALF):
        g = h // GROUP
        s = lax.dot_general(
            q_ref[:, h * HD : (h + 1) * HD],
            k_ref[:, g * HD : (g + 1) * HD],
            (((1,), (1,)), ((), ())),
            preferred_element_type=F32,
        )
        s = jnp.where(allowed, s * (HD**-0.5), -1e30)
        e = jnp.exp(s - jnp.max(s, axis=1, keepdims=True))
        p_ref[h] = (e / jnp.sum(e, axis=1, keepdims=True)).astype(BF16)


def attention(queries, keys, after):
    length = queries.shape[0]
    return whole(attention_kernel, shape(HALF, length, length, dtype=BF16), queries, keys, after)


def project_half(v_ref, gain_ref, x_ref, gvt_ref, core):
    low = left_lanes(8)
    total = jnp.zeros((32, x_ref.shape[0]), F32)
    for xi in range(4):
        for zp in range(4):
            row = (xi * 8 + 2 * zp) * 16
            quad = v_ref[row : row + 32].astype(F32)
            halves = []
            for h in range(2):
                one, two = quad[h * 8 : h * 8 + 8], quad[h * 8 + 16 : h * 8 + 24]
                halves.append(jnp.where(low, one, pltpu.roll(two, 64, 1)))
                halves.append(jnp.where(low, pltpu.roll(one, 64, 1), two))
            zero = (xi * 8 + zp) * 128
            gain = jnp.where(
                core == 0,
                gain_ref[:, zero : zero + 128].astype(F32),
                gain_ref[:, zero + 512 : zero + 640].astype(F32),
            )
            at = (xi * 4 + zp) * 128
            gvt_ref[:, at : at + 128] = (jnp.concatenate(halves, axis=0) * gain).astype(BF16)
        spot = pl.ds(pl.multiple_of(xi * 1024 + core * 512, 512), 512)
        total += lax.dot_general(
            gvt_ref[:, xi * 512 : (xi + 1) * 512],
            x_ref[:, spot],
            (((1,), (1,)), ((), ())),
            preferred_element_type=F32,
        )
    return total


def project_own_kernel(v_ref, gain_ref, x_ref, gvt_ref, u_ref):
    u_ref[...] = project_half(v_ref, gain_ref, x_ref, gvt_ref, lax.axis_index("core"))


def project_got_kernel(v_ref, gain_ref, x_ref, part_ref, ss_ref, gvt_ref, u_ref, send_ref):
    u = part_ref[...] + project_half(v_ref, gain_ref, x_ref, gvt_ref, 1 - lax.axis_index("core"))
    u_ref[...] = u[:HALF]
    send_ref[:HALF] = u[HALF:]
    send_ref[HALF:] = jnp.broadcast_to(ss_ref[...], (8, u.shape[1]))


def project(own, got, gain, x, ss):
    length, wide = x.shape
    half = shape(32, wide // 2, dtype=BF16)
    mine, part = whole(project_own_kernel, [half, shape(32, length)], own, gain, x)
    other, u, send = whole(
        project_got_kernel,
        [half, shape(HALF, length), shape(HALF + 8, length)],
        got, gain, x, part, ss,
    )
    return (mine, other), u, send


def values_kernel(width, p_ref, own_ref, got_ref, ss_ref, v_ref, u_ref, rms_ref):
    got = got_ref[...]
    rms = lax.rsqrt((ss_ref[...] + got[HALF : HALF + 1]) / width + EPS)
    rms_ref[...] = rms
    u = own_ref[...] + got[:HALF]
    u_ref[...] = u
    u = u * rms
    strips = []
    for row in range(0, p_ref.shape[1], 64):
        total = p_ref[0, row : row + 64].astype(F32) * u[:1]
        for j in range(1, HALF):
            total += p_ref[j, row : row + 64].astype(F32) * u[j : j + 1]
        strips.append(total)
    v_ref[...] = row_sum_of_transpose(jnp.concatenate(strips, axis=0))


def make_values(width, probs, own, got, ss):
    length = probs.shape[1]
    return whole(
        lambda *refs: values_kernel(width, *refs),
        [shape(1, length), shape(HALF, length), shape(1, length)],
        probs, own, got, ss,
    )


def error_kernel(p_ref, u_ref, own_ref, got_ref, targets_ref, scored_ref, values_ref, c_ref):
    length = u_ref.shape[1]
    values = own_ref[...] + got_ref[...]
    values_ref[...] = values
    error = (values - targets_ref[...]) * scored_ref[...].astype(F32)
    high = error.astype(BF16)
    low = (error - high.astype(F32)).astype(BF16)
    both = jnp.concatenate([jnp.broadcast_to(high, (8, length)), jnp.broadcast_to(low, (8, length))], axis=0)
    rows = []
    for j in range(HALF):
        c = jnp.dot(both, p_ref[j], preferred_element_type=F32)
        rows.append(c[:1] + c[8:9])
    c = jnp.concatenate(rows, axis=0)
    c_ref[:HALF] = c
    c_ref[HALF:] = jnp.broadcast_to(jnp.sum(c * u_ref[...], axis=0, keepdims=True), (8, length))


def make_error(probs, u, own, got, targets, scored):
    length = probs.shape[1]
    return whole(
        error_kernel, [shape(1, length), shape(HALF + 8, length)], probs, u, own, got, targets, scored
    )


def rows_kernel(own_ref, got_ref, rms_ref, x_ref, c_ref, dot_ref, keep_ref, send_ref):
    core = lax.axis_index("core")
    c = jnp.concatenate([own_ref[:HALF], got_ref[:HALF]], axis=0) * rms_ref[...]
    c_ref[...] = c
    dot_ref[...] = own_ref[HALF : HALF + 1] + got_ref[HALF : HALF + 1]
    high = c.astype(BF16)
    low = (c - high.astype(F32)).astype(BF16)
    both = jnp.concatenate([high, low], axis=0)
    z = jnp.dot(both, x_ref[...], preferred_element_type=F32)
    z = z[:32] + z[32:]
    left = left_lanes(8)

    def chunks(b):
        at = slice(b * 128, (b + 1) * 128)
        parts = [z[i * 8 : (i + 1) * 8, at] for i in range(4)]
        even = [jnp.where(left, parts[i], pltpu.roll(parts[i + 1], 64, 1)) for i in (0, 2)]
        odd = [jnp.where(left, pltpu.roll(parts[i], 64, 1), parts[i + 1]) for i in (0, 2)]
        return jnp.concatenate([*even, *odd], axis=0)

    for xi in range(4):
        for zp in range(4):
            at = pl.ds((xi * 4 + zp) * 32, 32)
            zero, one = chunks(xi * 8 + zp), chunks(xi * 8 + 4 + zp)
            keep_ref[at] = jnp.where(core == 0, zero, one)
            send_ref[at] = jnp.where(core == 0, one, zero).astype(BF16)


def make_rows(own, got, rms, x):
    length = x.shape[0]
    return whole(
        rows_kernel,
        [shape(32, length), shape(1, length), shape(512, 128), shape(512, 128, dtype=BF16)],
        own, got, rms, x,
    )


def sum_kernel(parts_ref, gain_ref, v_ref, w_ref, tails_ref):
    side = lax.axis_index("yl")
    xi, zi = lax.axis_index("x"), lax.axis_index("z")
    even = zi % 2 == 0
    v = v_ref[pl.ds(pl.multiple_of((xi * 8 + zi) * 16, 16), 16)].astype(F32)
    spot = (xi * 2 + lax.axis_index("core")) * 4 + zi // 2
    gain = jnp.zeros((1, 128), F32)
    for b in range(BLOCKS // 2):
        gain = jnp.where(spot == b, gain_ref[:, b * 128 : (b + 1) * 128].astype(F32), gain)
    gain = jnp.where(left_lanes(1) == even, gain, pltpu.roll(gain, 64, 1))
    total = jnp.zeros((HALF, 128), F32)
    for b in range(32):
        total += parts_ref[b].astype(F32)
    z = total * gain
    part = jnp.sum(total * v, axis=0, keepdims=True)
    part = jnp.broadcast_to(part + pltpu.roll(part, 64, 1), (8, 128))
    ws = [w_ref[i * ROWS : (i + 1) * ROWS] for i in range(4)]
    tails = []
    for h in range(2):
        rows = z[h * 8 : (h + 1) * 8]
        reads = []
        for g in range(2):
            reads.append(split_dot(rows[:, g * ROWS : (g + 1) * ROWS], ws[2 * h + g], ((1,), (0,))))
        tails.append(jnp.concatenate([*reads, part, rows], axis=0))
    for i in range(8):
        tails_ref[i] = jnp.where(side == i % 2, tails[0], tails[1]).astype(BF16)


def weight_kernel(z_ref, r_ref, grad_ref):
    for g in range(2):
        z = z_ref[:, g * ROWS : (g + 1) * ROWS]
        grad_ref[:, g * HD : (g + 1) * HD] = exact_dot(z, r_ref[g * GROUP : (g + 1) * GROUP], ((0,), (0,)))


def near_kernel(tails_ref, out_ref, z_ref):
    core, side, far = lax.axis_index("core"), lax.axis_index("yl"), lax.axis_index("yh")
    read = tails_ref[0].astype(F32)[:HALF]
    for i in range(1, 8):
        read += tails_ref[i].astype(F32)[:HALF]

    def pair(i):
        return tails_ref[i].astype(F32) + tails_ref[4 + i].astype(F32)

    zero, one = pair(side)[HALF : HALF + 8], pair(2 + side)[HALF : HALF + 8]
    z_ref[...] = pair(2 * core + far)[HALF + 8 :]
    tail = jnp.concatenate([read, jnp.where(left_lanes(8), zero, one)], axis=0).astype(BF16)
    for i in range(32):
        out_ref[i] = tail


def last_kernel(all_ref, read_ref, gain_ref):
    left = left_lanes(1)
    total = all_ref[0].astype(F32)
    for i in range(1, 32):
        total += all_ref[i].astype(F32)
    read_ref[...] = total[:HALF]
    for xi in range(4):
        for zp in range(4):
            i = xi * 8 + 2 * zp
            one = all_ref[i].astype(F32)[HALF : HALF + 1]
            two = all_ref[i + 1].astype(F32)[HALF : HALF + 1]
            row = xi * 8 + zp
            gain_ref[row : row + 1] = jnp.where(left, one, pltpu.roll(two, 64, 1))
            gain_ref[row + 4 : row + 5] = jnp.where(left, pltpu.roll(one, 64, 1), two)


def input_kernel(width, c_ref, dot_ref, rms_ref, mine_ref, other_ref, x_ref, after_ref, out_ref, log_ref):
    rms = rms_ref[...]
    length = rms.shape[1]
    c = c_ref[...]
    high = c.astype(BF16)
    low = (c - high.astype(F32)).astype(BF16)
    log_scale = rms * dot_ref[...]
    log_ref[...] = log_scale
    back = jnp.broadcast_to(rms * rms * log_scale / width, (128, length)).T
    first = lax.axis_index("core") == 0
    mine, other = mine_ref[...], other_ref[...]
    gvt = jnp.concatenate([jnp.where(first, mine, other), jnp.where(first, other, mine)], axis=1)
    grad = lax.dot_general(
        jnp.concatenate([high, low], axis=0),
        jnp.concatenate([gvt, gvt], axis=0),
        (((0,), (0,)), ((), ())),
        preferred_element_type=F32,
    )
    for b in range(grad.shape[1] // 128):
        at = slice(b * 128, (b + 1) * 128)
        out_ref[:, at] = (grad[:, at] - x_ref[:, at].astype(F32) * back).astype(BF16)


def input_grad(width, c, dot, rms, gvt, x, after):
    steps = 4
    length, wide = x.shape
    return pl.pallas_call(
        lambda *refs: input_kernel(width, *refs),
        grid=(steps,),
        in_specs=[
            pl.BlockSpec((32, length), lambda i: (0, 0)),
            pl.BlockSpec((1, length), lambda i: (0, 0)),
            pl.BlockSpec((1, length), lambda i: (0, 0)),
            pl.BlockSpec((32, wide // steps // 2), lambda i: (0, i)),
            pl.BlockSpec((32, wide // steps // 2), lambda i: (0, i)),
            pl.BlockSpec((length, wide // steps), lambda i: (0, i)),
            ANY,
        ],
        out_specs=[
            pl.BlockSpec((length, wide // steps), lambda i: (0, i)),
            pl.BlockSpec((1, length), lambda i: (0, 0)),
        ],
        out_shape=[shape(length, wide, dtype=BF16), shape(1, length)],
        compiler_params=PARAMS,
    )(c, dot, rms, *gvt, x, after)


def together(*values):
    return lax.optimization_barrier(values)


def shards(hidden_states, norm_gain, value_weight, queries, keys, readout, targets, scored):
    width = hidden_states.shape[1] * 2
    read = readout.reshape(HALF, HD)
    other_read = swap(read, "yl")
    ring = lax.ppermute(value_weight, ("yh", "yl"), [(1, 0), (0, 2), (2, 3), (3, 1)])
    pair = cross(value_weight)
    x, ss = load(hidden_states, norm_gain)
    ring, pair, ss = together(ring, pair, ss)
    weight, v = whole(
        choose_kernel, [shape(256, 128, dtype=BF16), shape(8, 128)], ring, pair, read
    )
    v, other_read = together(v, other_read)
    v = whole(read_kernel, shape(512, 128, dtype=BF16), weight, v, other_read)
    v = lax.all_to_all(v.reshape(32, HALF, 128), PLANE, 0, 0).reshape(512, 128)
    v, norm_gain, targets, scored = together(v, norm_gain, targets, scored)
    gain = norm_gain[None]
    gvt, u, send = project(v, swap(v, "core"), gain, x, ss)
    probs = attention(queries, keys, u)
    part, u, rms = make_values(width, probs, u, swap(send, "yl"), ss)
    got = swap(part, "yl")
    values, c = make_error(probs, u, part, got, targets[None], scored[None])
    c, dot, keep, send = make_rows(c, swap(c, "yl"), rms, x)
    z = (keep + swap(send, "core").astype(F32)).astype(BF16).reshape(32, HALF, 128)
    z = lax.all_to_all(z, PLANE, 0, 0)
    grad_input, log_scale = input_grad(width, c, dot, rms, gvt, x, z)
    tails = whole(sum_kernel, shape(8, HALF + 16, 128, dtype=BF16), z, gain, v, weight)
    tails = lax.all_to_all(tails, NEAR, 0, 0)
    tails, z = whole(near_kernel, [shape(32, HALF + 8, 128, dtype=BF16), shape(8, 128)], tails)
    grad_weight = whole(weight_kernel, shape(ROWS, 2 * HD), z, read)
    tails = lax.all_to_all(tails, PLANE, 0, 0)
    grad_readout, grad_gain = whole(last_kernel, [shape(HALF, HD), shape(32, 128)], tails)
    return (values[0], grad_input, grad_weight, grad_gain.reshape(-1), grad_readout.reshape(-1), log_scale[0])


def solution(mesh):
    fine = Mesh(mesh.devices.reshape(2, 4, 2, 8, 2), ("yh", "x", "core", "z", "yl"))
    seq = ("yh", "x", "core", "z")
    return jax.shard_map(
        shards,
        mesh=fine,
        in_specs=(
            P(seq, "yl"),
            P("yl"),
            P(seq, "yl"),
            P(seq, "yl"),
            P(seq, "yl"),
            P("yl"),
            P(seq),
            P(seq),
        ),
        out_specs=(
            P(seq),
            P(seq, "yl"),
            P(seq, "yl"),
            P("yl"),
            P("yl"),
            P(seq),
        ),
        check_vma=False,
    )
```
